256 devices in a mesh: ctx: 64 (over x, z, core), head: 4 (over y).
Axes of the slice: x: 4, y: 4, z: 8, core: 2. Of those that a mesh axis runs over, the one named last changes fastest.
Arguments:
- queries: bfloat16 [16384, 2560], P('ctx', 'head'), may hold values from -8 to 8
- key_tokens: bfloat16 [16384, 2560], P('ctx', 'head'), may hold values from -8 to 8
- value_tokens: bfloat16 [16384, 2560], P('ctx', 'head'), may hold values from -8 to 8
- pair_keys: int32 [512, 4], P('ctx'), may hold values from 0 to 511, as said below
- pair_count: int32 [512], P('ctx'), may hold values from 1 to 4, as said below
Outputs:
- attended: bfloat16 [16384, 2560], P('ctx', 'head')
The draws below stay inside these ranges and needn't reach their ends.
Inputs may be any that keep to these rules, and one draw needn't show every extreme that they name: `pair_keys`: the 4 entries of a row are distinct, padded slots too. Key block c lies on index c // 8 of ctx. Among all 4 slots (padded ones included) of the 8 rows of one index of ctx, at most 2 name key blocks of any one index, its own included, and on every index some one index is named exactly 2 times. `pair_count`: every index of ctx has a query block whose count is 4.
All inputs are finite; a program needn't handle non-finite values.
Results may differ from the reference program's by a relative error of at most 0.0059.
Values may be sent and summed in bfloat16 or wider, within the bound.
No kernel may reach another device: no remote copies, remote signals or barrier semaphores. Data moves between devices by JAX's collectives and lax.ppermute only.
A program may use at most 128 MiB of HBM per device.

```python
import math
import jax
import jax.numpy as jnp
from jax import lax

HD = 128
HEADS = 20
BLOCK = 32
PAIRS = 4
TOK_DEV = 256
TOKENS = 16384
NBLOCKS = 512
QB_DEV = 8
CAP = 2


def device_pairs(device_key):
    device_total = TOKENS // TOK_DEV
    slot_total = QB_DEV * PAIRS
    pool_total = device_total * CAP
    key_one, key_two, key_three, key_four = jax.random.split(device_key, 4)
    tile_owner = jnp.arange(pool_total, dtype=jnp.int32) // CAP
    forced_owner = jax.random.randint(key_one, (), 0, device_total)
    order_score = jnp.where(tile_owner == forced_owner, jnp.arange(pool_total, dtype=jnp.int32) - pool_total, jax.random.permutation(key_two, pool_total).astype(jnp.int32))
    ordering = jnp.argsort(order_score)
    owners = tile_owner[ordering][:slot_total]
    owners = owners[jax.random.permutation(key_three, slot_total)].reshape(QB_DEV, PAIRS)
    rotation = jax.random.permutation(key_four, QB_DEV)[:PAIRS].astype(jnp.int32)
    within = (jnp.arange(QB_DEV, dtype=jnp.int32)[:, None] + rotation[None, :]) % QB_DEV
    return owners * QB_DEV + within


def device_counts(device_key):
    key_one, key_two, key_three = jax.random.split(device_key, 3)
    ceiling = jax.random.randint(key_one, (), 1, PAIRS + 1)
    counts = jax.random.randint(key_two, (QB_DEV,), 1, ceiling + 1)
    forced_row = jax.random.randint(key_three, (), 0, QB_DEV)
    return counts.at[forced_row].set(PAIRS)


def trace_plan(key):
    device_total = TOKENS // TOK_DEV
    vector_key = jax.random.fold_in(key, 101)
    pair_key = jax.random.fold_in(key, 103)
    count_key = jax.random.fold_in(key, 107)
    block_vectors = jax.random.normal(vector_key, (NBLOCKS, HEADS * HD), jnp.float32)
    pair_table = jax.vmap(device_pairs)(jax.random.split(pair_key, device_total)).reshape(NBLOCKS, PAIRS)
    counts = jax.vmap(device_counts)(jax.random.split(count_key, device_total)).reshape(NBLOCKS)
    return (block_vectors, pair_table, counts)


def draw_queries(key, part):
    block_vectors, pair_table, counts = trace_plan(key)
    usable = (jnp.arange(PAIRS)[None, :] < counts[:, None]).astype(jnp.float32)
    direction = jnp.sum(block_vectors[pair_table] * usable[:, :, None], axis=1) * (2.2 / math.sqrt(HD))
    spread = jnp.repeat(direction, BLOCK, axis=0)
    own_key = jax.random.fold_in(key, 11)
    noise = jax.random.normal(own_key, (TOKENS, HEADS * HD), jnp.float32)
    result = jnp.clip(noise + spread, -8.0, 8.0)
    return result.astype(jnp.bfloat16)


def draw_key_tokens(key, part):
    block_vectors, pair_table, counts = trace_plan(key)
    spread = jnp.repeat(3.0 * block_vectors, BLOCK, axis=0)
    own_key = jax.random.fold_in(key, 13)
    noise = 1.2 * jax.random.normal(own_key, (TOKENS, HEADS * HD), jnp.float32)
    result = jnp.clip(spread + noise, -8.0, 8.0)
    return result.astype(jnp.bfloat16)


def draw_value_tokens(key, part):
    key = jax.random.fold_in(key, 17)
    block_key, token_key = jax.random.split(key)
    block_part = 0.8 * jax.random.normal(block_key, (NBLOCKS, HEADS * HD), jnp.float32)
    noise = 0.6 * jax.random.normal(token_key, (TOKENS, HEADS * HD), jnp.float32)
    result = jnp.clip(jnp.repeat(block_part, BLOCK, axis=0) + noise, -8.0, 8.0)
    return result.astype(jnp.bfloat16)


def draw_pair_keys(key, part):
    block_vectors, pair_table, counts = trace_plan(key)
    return pair_table


def draw_pair_count(key, part):
    block_vectors, pair_table, counts = trace_plan(key)
    return counts


def setup_inputs(seed: int = 0) -> dict:
    arg_keys = jax.random.split(jax.random.key(seed), 6)
    return {
        "queries": draw_queries(jax.random.fold_in(arg_keys[5], 71), 0),
        "key_tokens": draw_key_tokens(jax.random.fold_in(arg_keys[5], 71), 0),
        "value_tokens": draw_value_tokens(jax.random.fold_in(arg_keys[5], 71), 0),
        "pair_keys": draw_pair_keys(jax.random.fold_in(arg_keys[5], 71), 0),
        "pair_count": draw_pair_count(jax.random.fold_in(arg_keys[5], 71), 0),
    }


NEGATIVE = -1e+30

def reference(queries, key_tokens, value_tokens, pair_keys, pair_count):
    usable = jnp.arange(PAIRS, dtype=jnp.int32)[None, :] < pair_count[:, None]
    group = math.gcd(NBLOCKS, 32)
    group_steps = NBLOCKS // group
    inv_root = 1.0 / math.sqrt(HD)
    block_ids = jnp.arange(NBLOCKS, dtype=jnp.int32)

    def one_head(head_index):
        column_start = (head_index * HD).astype(jnp.int32)
        query_head = lax.dynamic_slice_in_dim(queries, column_start, HD, 1)
        key_head = lax.dynamic_slice_in_dim(key_tokens, column_start, HD, 1)
        value_head = lax.dynamic_slice_in_dim(value_tokens, column_start, HD, 1)
        key_blocks = key_head.reshape(NBLOCKS, BLOCK, HD)
        value_blocks = value_head.reshape(NBLOCKS, BLOCK, HD)
        key_means = lax.optimization_barrier(lax.optimization_barrier(jnp.mean(key_blocks.astype(jnp.float32), axis=1)).astype(jnp.bfloat16)).astype(jnp.float32)
        value_means = lax.optimization_barrier(lax.optimization_barrier(jnp.mean(value_blocks.astype(jnp.float32), axis=1)).astype(jnp.bfloat16)).astype(jnp.float32)
        query_blocks = query_head.reshape(NBLOCKS, BLOCK, HD)

        def group_fn(group_index):
            offset = (group_index * group).astype(jnp.int32)
            query_group = lax.dynamic_slice_in_dim(query_blocks, offset, group, 0).astype(jnp.float32)
            keys_group = lax.dynamic_slice_in_dim(pair_keys, offset, group, 0)
            usable_group = lax.dynamic_slice_in_dim(usable, offset, group, 0)
            refined = jnp.any((keys_group[:, :, None] == block_ids[None, None, :]) & usable_group[:, :, None], axis=1)
            coarse = jnp.einsum('gtd,cd->gtc', query_group, key_means, precision=lax.Precision.HIGHEST) * inv_root + math.log(BLOCK)
            coarse = jnp.where(refined[:, None, :], NEGATIVE, coarse)
            fine_keys = key_blocks[keys_group].astype(jnp.float32)
            fine_values = value_blocks[keys_group].astype(jnp.float32)
            fine = jnp.einsum('gtd,gpsd->gtps', query_group, fine_keys, precision=lax.Precision.HIGHEST) * inv_root
            fine = jnp.where(usable_group[:, None, :, None], fine, NEGATIVE)
            row_max = jnp.maximum(lax.optimization_barrier(jnp.max(coarse, axis=-1)), lax.optimization_barrier(jnp.max(fine, axis=(-2, -1))))
            coarse_weights = jnp.where(refined[:, None, :], 0.0, jnp.exp(coarse - row_max[..., None]))
            fine_weights = jnp.where(usable_group[:, None, :, None], jnp.exp(fine - row_max[..., None, None]), 0.0)
            denominator = lax.optimization_barrier(jnp.sum(coarse_weights, axis=-1)) + lax.optimization_barrier(jnp.sum(fine_weights, axis=(-2, -1)))
            coarse_rounded = lax.optimization_barrier(coarse_weights.astype(jnp.bfloat16)).astype(jnp.float32)
            fine_rounded = lax.optimization_barrier(fine_weights.astype(jnp.bfloat16)).astype(jnp.float32)
            numerator = jnp.einsum('gtc,cd->gtd', coarse_rounded, value_means, precision=lax.Precision.HIGHEST)
            numerator = numerator + jnp.einsum('gtps,gpsd->gtd', fine_rounded, fine_values, precision=lax.Precision.HIGHEST)
            return (numerator / denominator[..., None]).astype(jnp.bfloat16)
        result = lax.map(group_fn, jnp.arange(group_steps, dtype=jnp.int32))
        return result.reshape(TOKENS, HD)
    per_head = lax.map(one_head, jnp.arange(HEADS, dtype=jnp.int32))
    return jnp.transpose(per_head, (1, 0, 2)).reshape(TOKENS, HEADS * HD)
```

```python
import math

import jax
import jax.numpy as jnp
from jax import lax
from jax.experimental import pallas as pl
from jax.experimental.pallas import tpu as pltpu
from jax.sharding import PartitionSpec as P

HD = 128
BLOCK = 32
NEGATIVE = -1e30


def attend_kernel(
    half_blocks,
    pair_slots,
    pk_ref,
    pc_ref,
    q_ref,
    got_ref,
    mk_ref,
    mv_ref,
    o_ref,
    bias_ref,
):
    half, head = pl.program_id(0), pl.program_id(1)
    coarse_keys = mk_ref.shape[0]
    rows = got_ref.shape[1]
    fine_keys = BLOCK * rows
    inv_root = 1.0 / math.sqrt(HD)

    @pl.when(head == 0)
    def _():
        block_ids = lax.broadcasted_iota(jnp.int32, (1, coarse_keys), 1)
        row_ids = lax.broadcasted_iota(jnp.int32, (1, fine_keys), 1) % rows
        for local in range(half_blocks):
            block = half * half_blocks + local
            count = pc_ref[block]
            coarse = jnp.full((1, coarse_keys), math.log(BLOCK), jnp.float32)
            for slot in range(pair_slots):
                hit = jnp.where(slot < count, pk_ref[block * pair_slots + slot], -1)
                coarse = jnp.where(block_ids == hit, NEGATIVE, coarse)
            kept = (row_ids >= local * pair_slots) & (row_ids < local * pair_slots + count)
            fine = jnp.where(kept, 0.0, NEGATIVE)
            where = pl.ds(local * BLOCK, BLOCK)
            bias_ref[where, :coarse_keys] = jnp.broadcast_to(coarse, (BLOCK, coarse_keys))
            bias_ref[where, coarse_keys:] = jnp.broadcast_to(fine, (BLOCK, fine_keys))

    queries = q_ref[...]
    fine_k = got_ref[:BLOCK].reshape(fine_keys, HD)
    fine_v = got_ref[BLOCK:].reshape(fine_keys, HD)
    contract = (((1,), (1,)), ((), ()))
    coarse = lax.dot_general(queries, mk_ref[...], contract, preferred_element_type=jnp.float32)
    fine = lax.dot_general(queries, fine_k, contract, preferred_element_type=jnp.float32)
    coarse = coarse * inv_root + bias_ref[:, :coarse_keys]
    fine = fine * inv_root + bias_ref[:, coarse_keys:]
    top = jnp.maximum(
        jnp.max(coarse, axis=1, keepdims=True), jnp.max(fine, axis=1, keepdims=True)
    )
    coarse = jnp.exp(coarse - top)
    fine = jnp.exp(fine - top)
    total = jnp.sum(coarse, axis=1, keepdims=True) + jnp.sum(fine, axis=1, keepdims=True)
    numerator = jnp.dot(
        coarse.astype(jnp.bfloat16), mv_ref[...], preferred_element_type=jnp.float32
    )
    numerator = numerator + jnp.dot(
        fine.astype(jnp.bfloat16), fine_v, preferred_element_type=jnp.float32
    )
    o_ref[...] = (numerator / total).astype(o_ref.dtype)


def attend(queries, got, means, pair_keys, pair_count):
    tok_rows, columns = queries.shape
    heads = columns // HD
    block_count, pair_slots = pair_keys.shape
    halves = 2
    half_rows = tok_rows // halves
    half_slots = got.shape[1] // halves
    coarse_keys = means.shape[0]
    keys = coarse_keys + BLOCK * half_slots
    grid_spec = pltpu.PrefetchScalarGridSpec(
        num_scalar_prefetch=2,
        grid=(halves, heads),
        in_specs=[
            pl.BlockSpec((half_rows, HD), lambda i, h, *_: (i, h)),
            pl.BlockSpec((2 * BLOCK, half_slots, HD), lambda i, h, *_: (0, i, h)),
            pl.BlockSpec((coarse_keys, HD), lambda i, h, *_: (0, h)),
            pl.BlockSpec((coarse_keys, HD), lambda i, h, *_: (0, heads + h)),
        ],
        out_specs=pl.BlockSpec((half_rows, HD), lambda i, h, *_: (i, h)),
        scratch_shapes=[pltpu.VMEM((half_rows, keys), jnp.float32)],
    )

    def kernel(*refs):
        attend_kernel(block_count // halves, pair_slots, *refs)

    return pl.pallas_call(
        kernel,
        grid_spec=grid_spec,
        out_shape=jax.ShapeDtypeStruct((tok_rows, columns), jnp.bfloat16),
        compiler_params=pltpu.CompilerParams(vmem_limit_bytes=32 * 1024 * 1024),
        cost_estimate=pl.CostEstimate(
            flops=4 * tok_rows * keys * columns,
            bytes_accessed=8 * 1024 * 1024,
            transcendentals=tok_rows * keys * heads,
        ),
    )(pair_keys.reshape(-1), pair_count, queries, got, means, means)


def body(queries, key_tokens, value_tokens, pair_keys, pair_count):
    tok_rows, columns = queries.shape
    block_count = tok_rows // BLOCK
    pair_slots = pair_keys.shape[1]
    devices = lax.axis_size("ctx")
    blocks = devices * block_count
    assert devices == 2 * BLOCK

    key_blocks = key_tokens.reshape(block_count, BLOCK, columns)
    value_blocks = value_tokens.reshape(block_count, BLOCK, columns)
    key_means = jnp.mean(key_blocks.astype(jnp.float32), axis=1).astype(jnp.bfloat16)
    value_means = jnp.mean(value_blocks.astype(jnp.float32), axis=1).astype(jnp.bfloat16)
    means = lax.all_gather(
        jnp.concatenate((key_means, value_means), axis=1), "ctx", axis=0, tiled=True
    )

    by_row = jnp.concatenate(
        (jnp.transpose(key_blocks, (1, 0, 2)), jnp.transpose(value_blocks, (1, 0, 2))), axis=0
    )
    asked = jnp.concatenate((pair_keys // block_count, pair_keys % block_count), axis=1)
    asked = jnp.pad(asked.astype(jnp.bfloat16), ((0, 0), (0, HD - 2 * pair_slots)))
    asked = jnp.broadcast_to(asked[None], (devices, block_count, HD))
    spread = lax.all_to_all(
        jnp.concatenate((by_row, asked), axis=2), "ctx", split_axis=0, concat_axis=0, tiled=True
    )
    table = spread[:, :, :columns].reshape(blocks, columns)
    asked = spread[:, :, columns : columns + 2 * pair_slots].astype(jnp.int32)
    wanted = asked[:, :, :pair_slots] * block_count + asked[:, :, pair_slots:]
    choose = wanted.reshape(-1, 1) == jnp.arange(blocks, dtype=jnp.int32)[None, :]
    chosen = jnp.dot(choose.astype(jnp.bfloat16), table, preferred_element_type=jnp.float32)
    chosen = chosen.astype(jnp.bfloat16).reshape(devices, block_count * pair_slots, columns)
    got = lax.all_to_all(chosen, "ctx", split_axis=0, concat_axis=0, tiled=True)
    return attend(queries, got, means, pair_keys, pair_count)


def solution(mesh):
    placed = (P("ctx", "head"), P("ctx", "head"), P("ctx", "head"), P("ctx", None), P("ctx"))
    return jax.shard_map(
        body, mesh=mesh, in_specs=placed, out_specs=P("ctx", "head"), check_vma=False
    )
```

```python
import functools
import math

import jax
import jax.numpy as jnp
from jax import lax
from jax.experimental import pallas as pl
from jax.experimental.pallas import tpu as pltpu
from jax.sharding import PartitionSpec as P

HD = 128
BLOCK = 32
NX, NZ, NC = 4, 8, 2
NEGATIVE = -1e30
HALF = 128
EXTRA = 16
CAP = 2
MOST = CAP * NX * NC
FIRST = 2
CHUNK = 4
KEYS = 128
CONTRACT = (((1,), (1,)), ((), ()))
VMEM_LIMIT = 24 * 1024 * 1024


def shifted(dx, dz, dc):
    pairs = []
    for x in range(NX):
        for z in range(NZ):
            for c in range(NC):
                to = (((x + dx) % NX) * NZ + (z + dz) % NZ) * NC + (c ^ dc)
                pairs.append(((x * NZ + z) * NC + c, to))
    return pairs


def move(array, dx=0, dz=0, dc=0):
    return lax.ppermute(array, "ctx", shifted(dx, dz, dc))


def iota(shape, axis):
    return lax.broadcasted_iota(jnp.int32, shape, axis)


def spread_rows(table, first):
    rows = [jnp.broadcast_to(table[first + i : first + i + 1], (BLOCK, KEYS)) for i in range(4)]
    return jnp.concatenate(rows, axis=0)


def o_rows(half):
    return pl.ds(half * (HALF + EXTRA), HALF)


def pack_stats(tops, sums):
    lanes = iota((HALF, KEYS), 1)
    packed = jnp.zeros((HALF, KEYS), jnp.float32)
    heads = len(tops)
    for h in range(heads):
        high = sums[h].astype(jnp.bfloat16).astype(jnp.float32)
        packed = jnp.where(lanes == h, tops[h], packed)
        packed = jnp.where(lanes == heads + h, high, packed)
        packed = jnp.where(lanes == 2 * heads + h, sums[h] - high, packed)
    return jnp.transpose(packed)[:EXTRA].astype(jnp.bfloat16)


def unpack_stats(rows, heads):
    wide = jnp.concatenate(
        (rows.astype(jnp.float32), jnp.zeros((KEYS - EXTRA, HALF), jnp.float32)), axis=0
    )
    wide = jnp.transpose(wide)
    tops = [wide[:, h : h + 1] for h in range(heads)]
    sums = [
        wide[:, heads + h : heads + h + 1] + wide[:, 2 * heads + h : 2 * heads + h + 1]
        for h in range(heads)
    ]
    return tops, sums


def part_kernel(
    heads, slots, pos_ref, ids_ref, q_ref, *rest
):
    kv = rest[: NX * NC]
    out_ref, buf, means, acc, tops, sums, slot_b, slot_k, k_sem, v_sem, m_sem = rest[NX * NC :]
    mx, mz, mc = pos_ref[0], pos_ref[1], pos_ref[2]
    blocks = 2 * HALF // BLOCK
    tokens = blocks * BLOCK
    inv_root = 1.0 / math.sqrt(HD)

    def mean_copy(i):
        return pltpu.make_async_copy(
            kv[i].at[pl.ds(2 * tokens, EXTRA)], means.at[i], m_sem.at[i]
        )

    for i in range(NX * NC):
        mean_copy(i).start()

    def copies(source, within, n):
        first = pl.multiple_of(within * BLOCK, BLOCK)
        return (
            pltpu.make_async_copy(
                source.at[pl.ds(first, BLOCK)], buf.at[n, pl.ds(0, BLOCK)], k_sem.at[n]
            ),
            pltpu.make_async_copy(
                source.at[pl.ds(tokens + first, BLOCK)], buf.at[n, pl.ds(BLOCK, BLOCK)], v_sem.at[n]
            ),
        )

    def ask(t, n):
        b, p = t // slots, t % slots
        owner = ids_ref[b * 16 + p]
        within = ids_ref[b * 16 + slots + p]
        count = ids_ref[b * 16 + 2 * slots]
        here = (p < count) & (((owner >> 1) & (NZ - 1)) == mz)

        @pl.when(here)
        def _():
            rel = (((owner >> 4) - mx) & (NX - 1)) * NC + ((owner & 1) ^ mc)
            slot_b[n] = b
            slot_k[n] = rel * blocks + within
            for i in range(NX * NC):

                @pl.when(rel == i)
                def _(i=i):
                    for copy in copies(kv[i], within, n):
                        copy.start()

        return n + here.astype(jnp.int32)

    used = lax.fori_loop(0, blocks * slots, ask, jnp.int32(0))
    chunks = (jnp.maximum(used - FIRST, 0) + CHUNK - 1) // CHUNK

    def blank(n, carry):
        slot_b[n] = -1
        slot_k[n] = -1
        buf[n] = jnp.zeros(buf.shape[1:], buf.dtype)
        return carry

    lax.fori_loop(used, FIRST + CHUNK * chunks, blank, 0)

    def arrived(n):
        @pl.when(n < used)
        def _():
            for copy in copies(kv[0], 0, n):
                copy.wait()

    block_ids, lanes = iota((blocks, KEYS), 0), iota((blocks, KEYS), 1)

    def exclude(n, table):
        return jnp.where((block_ids == slot_b[n]) & (lanes == slot_k[n]), NEGATIVE, table)

    bias = jnp.full((blocks, KEYS), math.log(BLOCK), jnp.float32)
    bias = lax.fori_loop(0, used, exclude, bias)
    for j in range(FIRST):
        mine = jnp.where(block_ids == slot_b[j], 0.0, NEGATIVE)
        bias = jnp.where(lanes >= KEYS - (FIRST - j) * BLOCK, mine, bias)
    for i in range(NX * NC):
        mean_copy(i).wait()
    for j in range(FIRST):
        arrived(j)
    for h in range(heads):
        cols = pl.ds(h * HD, HD)
        tiles = [means[i, :, cols].astype(jnp.float32) for i in range(NX * NC)]
        mean_k = jnp.concatenate([t[:8] for t in tiles], axis=0).astype(jnp.bfloat16)
        mean_v = jnp.concatenate([t[8:] for t in tiles], axis=0).astype(jnp.bfloat16)
        keys = jnp.concatenate([mean_k] + [buf[j, :BLOCK, cols] for j in range(FIRST)], axis=0)
        values = jnp.concatenate([mean_v] + [buf[j, BLOCK:, cols] for j in range(FIRST)], axis=0)
        for half in range(2):
            where = pl.ds(half * HALF, HALF)
            logits = lax.dot_general(
                q_ref[o_rows(half), cols], keys, CONTRACT, preferred_element_type=jnp.float32
            )
            logits = logits * inv_root + spread_rows(bias, half * 4)
            top = jnp.max(logits, axis=1, keepdims=True)
            weights = jnp.exp(logits - top)
            tops[where, cols] = jnp.broadcast_to(top, (HALF, HD))
            sums[where, cols] = jnp.broadcast_to(
                jnp.sum(weights, axis=1, keepdims=True), (HALF, HD)
            )
            acc[where, cols] = jnp.dot(
                weights.astype(jnp.bfloat16), values, preferred_element_type=jnp.float32
            )

    def chunk(ci, carry):
        first = FIRST + ci * CHUNK
        table = jnp.full((blocks, KEYS), NEGATIVE, jnp.float32)
        for j in range(CHUNK):
            arrived(first + j)
            mine = jnp.where(block_ids == slot_b[first + j], 0.0, NEGATIVE)
            table = jnp.where(lanes // BLOCK == j, mine, table)
        for h in range(heads):
            cols = pl.ds(h * HD, HD)
            keys = jnp.concatenate([buf[first + j, :BLOCK, cols] for j in range(CHUNK)], axis=0)
            values = jnp.concatenate([buf[first + j, BLOCK:, cols] for j in range(CHUNK)], axis=0)
            for half in range(2):
                where = pl.ds(half * HALF, HALF)
                logits = lax.dot_general(
                    q_ref[o_rows(half), cols], keys, CONTRACT, preferred_element_type=jnp.float32
                )
                logits = logits * inv_root + spread_rows(table, half * 4)
                before = tops[where, cols]
                top = jnp.maximum(before, jnp.max(logits, axis=1, keepdims=True))
                weights = jnp.exp(logits - top)
                ratio = jnp.exp(before - top)
                tops[where, cols] = top
                sums[where, cols] = sums[where, cols] * ratio + jnp.sum(
                    weights, axis=1, keepdims=True
                )
                acc[where, cols] = acc[where, cols] * ratio + jnp.dot(
                    weights.astype(jnp.bfloat16), values, preferred_element_type=jnp.float32
                )
        return carry

    lax.fori_loop(0, chunks, chunk, 0)

    stats = []
    for half in range(2):
        where = pl.ds(half * HALF, HALF)
        sent_tops, sent_sums = [], []
        for h in range(heads):
            cols = pl.ds(h * HD, HD)
            top = tops[where, cols]
            sent = top.astype(jnp.bfloat16).astype(jnp.float32)
            factor = jnp.exp(top - sent)
            sent_tops.append(sent)
            sent_sums.append(sums[where, cols] * factor)
            out_ref[o_rows(half), cols] = (acc[where, cols] * factor).astype(out_ref.dtype)
        stats.append(pack_stats(sent_tops, sent_sums))
    out_ref[HALF : HALF + EXTRA, : 2 * HALF] = jnp.concatenate(stats, axis=1)
    rest_cols = out_ref.shape[1] - 2 * HALF
    out_ref[HALF : HALF + EXTRA, 2 * HALF :] = jnp.zeros((EXTRA, rest_cols), out_ref.dtype)


def part(position, query_pay, kv):
    rows, columns = query_pay.shape
    heads = columns // HD
    slots = 4
    ids = query_pay[HALF : HALF + 8, :16].astype(jnp.int32).reshape(-1)
    wanted = FIRST + MOST
    any_space = pl.BlockSpec(memory_space=pl.ANY)
    grid_spec = pltpu.PrefetchScalarGridSpec(
        num_scalar_prefetch=2,
        grid=(1,),
        in_specs=[pl.BlockSpec((rows, columns), lambda i, *_: (0, 0))] + [any_space] * len(kv),
        out_specs=pl.BlockSpec((rows, columns), lambda i, *_: (0, 0)),
        scratch_shapes=[
            pltpu.VMEM((wanted, 2 * BLOCK, columns), jnp.bfloat16),
            pltpu.VMEM((len(kv), EXTRA, columns), jnp.bfloat16),
            pltpu.VMEM((2 * HALF, columns), jnp.float32),
            pltpu.VMEM((2 * HALF, columns), jnp.float32),
            pltpu.VMEM((2 * HALF, columns), jnp.float32),
            pltpu.SMEM((wanted,), jnp.int32),
            pltpu.SMEM((wanted,), jnp.int32),
            pltpu.SemaphoreType.DMA((wanted,)),
            pltpu.SemaphoreType.DMA((wanted,)),
            pltpu.SemaphoreType.DMA((len(kv),)),
        ],
    )
    return pl.pallas_call(
        functools.partial(part_kernel, heads, slots),
        grid_spec=grid_spec,
        out_shape=jax.ShapeDtypeStruct((rows, columns), jnp.bfloat16),
        compiler_params=pltpu.CompilerParams(vmem_limit_bytes=VMEM_LIMIT),
        cost_estimate=pl.CostEstimate(
            flops=4 * 256 * 1024 * columns, bytes_accessed=4 * 1024 * 1024, transcendentals=500000
        ),
    )(position, ids, query_pay, *kv)


def merge_parts(heads, half, parts):
    cols_of_half = pl.ds(half * HALF, HALF)
    unpacked = [
        unpack_stats(ref[pl.ds(stat_row, EXTRA), cols_of_half], heads)
        for ref, _, stat_row in parts
    ]
    tops, totals, sums = [], [], []
    for h in range(heads):
        cols = pl.ds(h * HD, HD)
        wide = [jnp.broadcast_to(u[0][h], (HALF, HD)) for u in unpacked]
        top = functools.reduce(jnp.maximum, wide)
        total = jnp.zeros((HALF, HD), jnp.float32)
        numerator = jnp.zeros((HALF, HD), jnp.float32)
        for (ref, row, _), u, w in zip(parts, unpacked, wide):
            ratio = jnp.exp(w - top)
            total = total + ratio * u[1][h]
            numerator = numerator + ratio * ref[pl.ds(row, HALF), cols].astype(jnp.float32)
        tops.append(top)
        totals.append(total)
        sums.append(numerator)
    return tops, totals, sums


def write_half(heads, half, out_ref, merged):
    tops, totals, sums = merged
    for h in range(heads):
        out_ref[o_rows(half), pl.ds(h * HD, HD)] = sums[h].astype(out_ref.dtype)
    out_ref[HALF : HALF + EXTRA, half * HALF : (half + 1) * HALF] = pack_stats(tops, totals)


def merge_kernel(heads, halves, up_ref, up_in_ref, down_ref, down_in_ref, up_out, down_out):
    second = HALF + EXTRA
    for ref, in_ref, out_ref, upward in (
        (up_ref, up_in_ref, up_out, True),
        (down_ref, down_in_ref, down_out, False),
    ):
        out_ref[HALF:second, :] = ref[HALF:second, :]
        for half in range(2):
            row = half * second
            if not halves:
                parts = [(ref, row, HALF), (in_ref, row, HALF)]
            elif upward and half == 0:
                parts = [(ref, row, HALF), (in_ref, 0, HALF)]
            elif not upward and half == 1:
                parts = [(ref, row, HALF), (in_ref, EXTRA, 0)]
            else:
                out_ref[o_rows(half), :] = ref[o_rows(half), :]
                continue
            write_half(heads, half, out_ref, merge_parts(heads, half, parts))


def merge(halves, up, up_in, down, down_in):
    rows, columns = up.shape
    whole = jax.ShapeDtypeStruct((rows, columns), jnp.bfloat16)
    return pl.pallas_call(
        functools.partial(merge_kernel, columns // HD, halves),
        out_shape=(whole, whole),
        compiler_params=pltpu.CompilerParams(vmem_limit_bytes=VMEM_LIMIT),
        cost_estimate=pl.CostEstimate(
            flops=1000000, bytes_accessed=2 * 1024 * 1024, transcendentals=1000
        ),
    )(up, up_in, down, down_in)


def last_kernel(heads, own_ref, up_ref, down_ref, out_ref):
    for half in range(2):
        row = half * (HALF + EXTRA)
        parts = [(ref, row, HALF) for ref in (own_ref, up_ref, down_ref)]
        _, totals, sums = merge_parts(heads, half, parts)
        for h in range(heads):
            out_ref[pl.ds(half * HALF, HALF), pl.ds(h * HD, HD)] = (sums[h] / totals[h]).astype(
                out_ref.dtype
            )


def last(own, up, down):
    rows, columns = own.shape
    return pl.pallas_call(
        functools.partial(last_kernel, columns // HD),
        out_shape=jax.ShapeDtypeStruct((2 * HALF, columns), jnp.bfloat16),
        compiler_params=pltpu.CompilerParams(vmem_limit_bytes=VMEM_LIMIT),
    )(own, up, down)


def body(queries, key_tokens, value_tokens, pair_keys, pair_count):
    tok_rows, columns = queries.shape
    blocks = tok_rows // BLOCK
    slots = pair_keys.shape[1]
    assert lax.axis_size("ctx") == NX * NZ * NC and tok_rows == 2 * HALF
    me = lax.axis_index("ctx")
    position = jnp.stack((me // (NZ * NC), (me // NC) % NZ, me % NC)).astype(jnp.int32)

    asked = jnp.concatenate(
        (pair_keys // blocks, pair_keys % blocks, pair_count[:, None]), axis=1
    ).astype(jnp.bfloat16)
    asked = jnp.pad(asked, ((0, EXTRA - blocks), (0, columns - 2 * slots - 1)))
    pay = jnp.concatenate((queries[:HALF], asked, queries[HALF:]), axis=0)

    def means(tokens):
        grouped = tokens.reshape(blocks, BLOCK, columns).astype(jnp.float32)
        return jnp.mean(grouped, axis=1).astype(jnp.bfloat16)

    own = jnp.concatenate(
        (key_tokens, value_tokens, means(key_tokens), means(value_tokens)), axis=0
    )
    plane = [own, move(own, dx=-1), move(own, dx=2), move(own, dx=1)]
    kv = []
    for there in plane:
        kv += [there, move(there, dc=1)]

    up, down = [pay], [pay]
    for _ in range(3):
        up.append(move(up[-1], dz=1))
        down.append(move(down[-1], dz=-1))
    far_up = move(up[3][: HALF + EXTRA], dz=1)
    far_down = move(down[3][HALF:], dz=-1)
    far = jnp.concatenate((far_up, far_down[EXTRA:]), axis=0)

    far_part = part(position, far, kv)
    up_in = move(far_part[: HALF + EXTRA], dz=-1)
    down_in = move(far_part[HALF:], dz=1)
    for hop in (3, 2, 1):
        up_part = part(position, up[hop], kv)
        down_part = part(position, down[hop], kv)
        up_sum, down_sum = merge(hop == 3, up_part, up_in, down_part, down_in)
        up_in = move(up_sum, dz=-1)
        down_in = move(down_sum, dz=1)
    own_part = part(position, pay, kv)
    return last(own_part, up_in, down_in)


def solution(mesh):
    placed = (P("ctx", "head"), P("ctx", "head"), P("ctx", "head"), P("ctx", None), P("ctx"))
    return jax.shard_map(
        body, mesh=mesh, in_specs=placed, out_specs=P("ctx", "head"), check_vma=False
    )
```

```python
import functools
import math

import jax
import jax.numpy as jnp
from jax import lax
from jax.experimental import pallas as pl
from jax.experimental.pallas import tpu as pltpu
from jax.sharding import PartitionSpec as P

HD = 128
BLOCK = 32
NX, NZ, NC = 4, 8, 2
BLOCKS = 8
SLOTS = 4
TOKENS = BLOCKS * BLOCK
HALF = TOKENS // 2
REQUEST = 16
STATS = 32
MEANS = 16
PLANE = NX * NC
MOST = 2 * PLANE
FIRST = 2
CHUNK = 4
NEGATIVE = -1e30
ROWS_ROWS = (((1,), (1,)), ((), ()))
COLS_COLS = (((0,), (0,)), ((), ()))
PARAMS = pltpu.CompilerParams(vmem_limit_bytes=24 * 1024 * 1024)


def move(array, dx=0, dz=0, dc=0):
    pairs = []
    for x in range(NX):
        for z in range(NZ):
            for c in range(NC):
                to = (((x + dx) % NX) * NZ + (z + dz) % NZ) * NC + (c ^ dc)
                pairs.append(((x * NZ + z) * NC + c, to))
    return lax.ppermute(array, "ctx", pairs)


def iota(shape, axis):
    return lax.broadcasted_iota(jnp.int32, shape, axis)


def part_kernel(heads, groups, pos_ref, ids_ref, mk_ref, mv_ref, *rest):
    count = len(groups)
    q_refs, rest = rest[:count], rest[count:]
    key_refs, rest = rest[:PLANE], rest[PLANE:]
    value_refs, rest = rest[:PLANE], rest[PLANE:]
    out_refs, rest = rest[:count], rest[count:]
    bufs, rest = rest[:count], rest[count:]
    accs, rest = rest[:count], rest[count:]
    tops, rest = rest[:count], rest[count:]
    sums, rest = rest[:count], rest[count:]
    biases, rest = rest[:count], rest[count:]
    slot_b, slot_k, k_sem, v_sem = rest
    mx, mz, mc = pos_ref[0], pos_ref[1], pos_ref[2]
    inv_root = 1.0 / math.sqrt(HD)

    def copies(g, i, within, n):
        first = pl.multiple_of(within * BLOCK, BLOCK)
        value_first = value_refs[i].shape[0] - TOKENS + first
        return (
            pltpu.make_async_copy(
                key_refs[i].at[pl.ds(first, BLOCK)], bufs[g].at[n, pl.ds(0, BLOCK)], k_sem.at[g, n]
            ),
            pltpu.make_async_copy(
                value_refs[i].at[pl.ds(pl.multiple_of(value_first, 16), BLOCK)],
                bufs[g].at[n, pl.ds(BLOCK, BLOCK)],
                v_sem.at[g, n],
            ),
        )

    useds = []
    for g, (_, low, blocks, place) in enumerate(groups):

        def ask(b, n, g=g, place=place):
            base = place * BLOCKS * 16 + b * 16
            limit = ids_ref[base + 2 * SLOTS]
            for p in range(SLOTS):
                owner = ids_ref[base + p]
                here = (p < limit) & (((owner >> 1) & (NZ - 1)) == mz)

                @pl.when(here)
                def _(n=n, p=p, owner=owner):
                    within = ids_ref[base + SLOTS + p]
                    rel = (((owner >> 4) - mx) & (NX - 1)) * NC + ((owner & 1) ^ mc)
                    slot_b[g, n] = b
                    slot_k[g, n] = rel * BLOCKS + within
                    for i in range(PLANE):

                        @pl.when(rel == i)
                        def _(i=i):
                            for copy in copies(g, i, within, n):
                                copy.start()

                n = n + here.astype(jnp.int32)
            return n

        useds.append(lax.fori_loop(low, low + blocks, ask, jnp.int32(0)))

    def arrived(g, n):
        @pl.when(n < useds[g])
        def _():
            for copy in copies(g, 0, 0, n):
                copy.wait()

    def q_of(g, cols):
        pieces = [q_refs[g][row : row + HALF, cols] for row in groups[g][0]]
        return pieces[0] if len(pieces) == 1 else jnp.concatenate(pieces, axis=0)

    chunks = []
    for g, (_, low, blocks, _) in enumerate(groups):
        tokens = blocks * BLOCK
        used = useds[g]
        chunks.append((jnp.maximum(used - FIRST, 0) + CHUNK - 1) // CHUNK)

        def blank(n, carry, g=g):
            slot_b[g, n] = -1
            bufs[g][n] = jnp.zeros(bufs[g].shape[1:], bufs[g].dtype)
            return carry

        lax.fori_loop(used, FIRST + CHUNK * chunks[g], blank, 0)
        shape = (PLANE * BLOCKS, tokens)
        key_ids, token_blocks = iota(shape, 0), iota(shape, 1) // BLOCK + low

        def exclude(n, table, g=g, key_ids=key_ids, token_blocks=token_blocks):
            hit = (key_ids == slot_k[g, n]) & (token_blocks == slot_b[g, n])
            return jnp.where(hit, NEGATIVE, table)

        bias = jnp.full(shape, math.log(BLOCK), jnp.float32)
        biases[g][...] = lax.fori_loop(0, used, exclude, bias)

    def slot_bias(g, n):
        _, low, blocks, _ = groups[g]
        token_blocks = iota((1, blocks * BLOCK), 1) // BLOCK + low
        return jnp.where(token_blocks == slot_b[g, n], 0.0, NEGATIVE)

    for g in range(count):
        for j in range(FIRST):
            arrived(g, j)
        slot_rows = [slot_bias(g, j) for j in range(FIRST)]
        tokens = groups[g][2] * BLOCK
        for h in range(heads):
            cols = pl.ds(h * HD, HD)
            keys = [mk_ref[:, cols]] + [bufs[g][j, :BLOCK, cols] for j in range(FIRST)]
            values = [mv_ref[:, cols]] + [bufs[g][j, BLOCK:, cols] for j in range(FIRST)]
            logits = lax.dot_general(
                jnp.concatenate(keys, axis=0),
                q_of(g, cols),
                ROWS_ROWS,
                preferred_element_type=jnp.float32,
            )
            logits = logits * inv_root
            first = PLANE * BLOCKS
            pieces = [logits[:first] + biases[g][...]]
            for j in range(FIRST):
                pieces.append(logits[first + j * BLOCK : first + (j + 1) * BLOCK] + slot_rows[j])
            logits = jnp.concatenate(pieces, axis=0)
            top = jnp.max(logits, axis=0, keepdims=True)
            weights = jnp.exp(logits - top)
            tops[g][h : h + 1] = top
            sums[g][h : h + 1] = jnp.sum(weights, axis=0, keepdims=True)
            accs[g][cols] = lax.dot_general(
                jnp.concatenate(values, axis=0),
                weights.astype(jnp.bfloat16),
                COLS_COLS,
                preferred_element_type=jnp.float32,
            )

    for g in range(count):

        def chunk(ci, carry, g=g):
            first = FIRST + ci * CHUNK
            for j in range(CHUNK):
                arrived(g, first + j)
            slot_rows = [slot_bias(g, first + j) for j in range(CHUNK)]
            for h in range(heads):
                cols = pl.ds(h * HD, HD)
                keys = [bufs[g][first + j, :BLOCK, cols] for j in range(CHUNK)]
                values = [bufs[g][first + j, BLOCK:, cols] for j in range(CHUNK)]
                logits = lax.dot_general(
                    jnp.concatenate(keys, axis=0),
                    q_of(g, cols),
                    ROWS_ROWS,
                    preferred_element_type=jnp.float32,
                )
                logits = logits * inv_root
                pieces = [
                    logits[j * BLOCK : (j + 1) * BLOCK] + slot_rows[j] for j in range(CHUNK)
                ]
                logits = jnp.concatenate(pieces, axis=0)
                before = tops[g][h : h + 1]
                top = jnp.maximum(before, jnp.max(logits, axis=0, keepdims=True))
                weights = jnp.exp(logits - top)
                ratio = jnp.exp(before - top)
                tops[g][h : h + 1] = top
                sums[g][h : h + 1] = sums[g][h : h + 1] * ratio + jnp.sum(
                    weights, axis=0, keepdims=True
                )
                accs[g][cols] = accs[g][cols] * ratio + lax.dot_general(
                    jnp.concatenate(values, axis=0),
                    weights.astype(jnp.bfloat16),
                    COLS_COLS,
                    preferred_element_type=jnp.float32,
                )
            return carry

        lax.fori_loop(0, chunks[g], chunk, 0)

    for g in range(count):
        top = tops[g][...]
        sent = top.astype(jnp.bfloat16).astype(jnp.float32)
        factor = jnp.exp(top - sent)
        for h in range(heads):
            cols = pl.ds(h * HD, HD)
            out_refs[g][cols] = (accs[g][cols] * factor[h : h + 1]).astype(jnp.bfloat16)
        write_stats(out_refs[g], slice(None), heads, sent, sums[g][...] * factor)


def write_stats(out_ref, lanes, heads, top, total):
    high = total.astype(jnp.bfloat16).astype(jnp.float32)
    rows = (top, high, total - high, jnp.zeros_like(top))
    valid = iota(top.shape, 0) < heads
    rows = [jnp.where(valid, r, 0.0) for r in rows]
    out_ref[heads * HD :, lanes] = jnp.concatenate(rows, axis=0).astype(jnp.bfloat16)


def part(position, ids, mean_k, mean_v, key_refs, value_refs, queries, groups):
    columns = mean_k.shape[1]
    heads = columns // HD
    wanted = FIRST + MOST
    vmem = pl.BlockSpec(memory_space=pltpu.VMEM)
    smem = pl.BlockSpec(memory_space=pltpu.SMEM)
    hbm = pl.BlockSpec(memory_space=pl.ANY)
    widths = [group[2] * BLOCK for group in groups]
    count = len(groups)
    scratch = [pltpu.VMEM((wanted, 2 * BLOCK, columns), jnp.bfloat16)] * count
    scratch += [pltpu.VMEM((columns, w), jnp.float32) for w in widths]
    scratch += [pltpu.VMEM((8, w), jnp.float32) for w in widths] * 2
    scratch += [pltpu.VMEM((PLANE * BLOCKS, w), jnp.float32) for w in widths]
    scratch += [pltpu.SMEM((count, wanted), jnp.int32)] * 2
    scratch += [pltpu.SemaphoreType.DMA((count, wanted))] * 2
    return pl.pallas_call(
        functools.partial(part_kernel, heads, groups),
        in_specs=[smem, smem, vmem, vmem] + [vmem] * count + [hbm] * (2 * PLANE),
        out_specs=[vmem] * count,
        out_shape=[jax.ShapeDtypeStruct((columns + STATS, w), jnp.bfloat16) for w in widths],
        scratch_shapes=scratch,
        compiler_params=PARAMS,
        cost_estimate=pl.CostEstimate(
            flops=4 * 512 * 1024 * columns, bytes_accessed=4 * 1024 * 1024, transcendentals=500000
        ),
    )(position, ids, mean_k, mean_v, *queries, *key_refs, *value_refs)


def stats_of(ref, lanes, heads):
    rows = ref[heads * HD :, lanes].astype(jnp.float32)
    return rows[:8], rows[8:16] + rows[16:24]


def merged(heads, parts):
    stats = [stats_of(ref, lanes, heads) for ref, lanes in parts]
    top = functools.reduce(jnp.maximum, [s[0] for s in stats])
    ratios = [jnp.exp(s[0] - top) for s in stats]
    total = functools.reduce(jnp.add, [r * s[1] for r, s in zip(ratios, stats)])
    return top, ratios, total


def merge_kernel(heads, up_ref, up_in_ref, down_ref, down_in_ref, up_out, down_out):
    for own, came, out, up in (
        (up_ref, up_in_ref, up_out, True),
        (down_ref, down_in_ref, down_out, False),
    ):
        width = came.shape[1]
        if width == own.shape[1]:
            lanes = slice(None)
        else:
            lanes = slice(0, width) if up else slice(width, 2 * width)
            rest = slice(width, 2 * width) if up else slice(0, width)
            out[:, rest] = own[:, rest]
        top, ratios, total = merged(heads, ((own, lanes), (came, slice(None))))
        for h in range(heads):
            cols = pl.ds(h * HD, HD)
            one = own[cols, lanes].astype(jnp.float32) * ratios[0][h : h + 1]
            two = came[cols, :].astype(jnp.float32) * ratios[1][h : h + 1]
            out[cols, lanes] = (one + two).astype(jnp.bfloat16)
        write_stats(out, lanes, heads, top, total)


def merge(up, up_in, down, down_in):
    heads = (up.shape[0] - STATS) // HD
    whole = jax.ShapeDtypeStruct(up.shape, jnp.bfloat16)
    return pl.pallas_call(
        functools.partial(merge_kernel, heads),
        out_shape=(whole, whole),
        compiler_params=PARAMS,
        cost_estimate=pl.CostEstimate(
            flops=1000000, bytes_accessed=2 * 1024 * 1024, transcendentals=1000
        ),
    )(up, up_in, down, down_in)


def last_kernel(heads, own_ref, up_ref, down_ref, out_ref):
    refs = (own_ref, up_ref, down_ref)
    _, ratios, total = merged(heads, [(ref, slice(None)) for ref in refs])
    valid = iota(total.shape, 0) < heads
    scales = [r / jnp.where(valid, total, 1.0) for r in ratios]
    for h in range(heads):
        cols = pl.ds(h * HD, HD)
        whole = jnp.zeros((HD, TOKENS), jnp.float32)
        for ref, scale in zip(refs, scales):
            whole = whole + ref[cols].astype(jnp.float32) * scale[h : h + 1]
        out_ref[:, cols] = jnp.transpose(whole).astype(out_ref.dtype)


def last(own, up, down):
    columns = own.shape[0] - STATS
    return pl.pallas_call(
        functools.partial(last_kernel, columns // HD),
        out_shape=jax.ShapeDtypeStruct((TOKENS, columns), jnp.bfloat16),
        compiler_params=PARAMS,
    )(own, up, down)


def ids_of(pay):
    return pay[HALF : HALF + BLOCKS, :16].astype(jnp.int32).reshape(-1)


def body(queries, key_tokens, value_tokens, pair_keys, pair_count):
    tok_rows, columns = queries.shape
    assert lax.axis_size("ctx") == NX * NZ * NC
    assert tok_rows == TOKENS and pair_keys.shape == (BLOCKS, SLOTS)
    me = lax.axis_index("ctx")
    position = jnp.stack((me // (NZ * NC), (me // NC) % NZ, me % NC)).astype(jnp.int32)
    barrier = lax.optimization_barrier

    asked = jnp.concatenate(
        (pair_keys // BLOCKS, pair_keys % BLOCKS, pair_count[:, None]), axis=1
    ).astype(jnp.bfloat16)
    asked = jnp.pad(asked, ((0, REQUEST - BLOCKS), (0, columns - 2 * SLOTS - 1)))
    pay = jnp.concatenate((queries[:HALF], asked, queries[HALF:]), axis=0)

    def means(tokens):
        grouped = tokens.reshape(BLOCKS, BLOCK, columns).astype(jnp.float32)
        return jnp.mean(grouped, axis=1).astype(jnp.bfloat16)

    split = TOKENS + MEANS
    own = jnp.concatenate(
        (key_tokens, means(key_tokens), means(value_tokens), value_tokens), axis=0
    )
    pay, own = barrier((pay, own))
    up1, down1 = move(pay, dz=1), move(pay, dz=-1)
    left, right = move(own, dx=1), move(own, dx=-1)
    own_twin = move(own, dc=1)
    up1, down1, left, right, own_twin = barrier((up1, down1, left, right, own_twin))

    up2, down2 = move(up1, dz=1), move(down1, dz=-1)
    far_k, far_v = move(left[:split], dx=1), move(right[split:], dx=-1)
    left_twin, right_twin = move(left, dc=1), move(right, dc=1)
    up2, down2, far_k, far_v, left_twin, right_twin = barrier(
        (up2, down2, far_k, far_v, left_twin, right_twin)
    )

    up3, down3 = move(up2, dz=1), move(down2, dz=-1)
    far_k_twin, far_v_twin = move(far_k, dc=1), move(far_v, dc=1)
    up3, down3, far_k_twin, far_v_twin = barrier((up3, down3, far_k_twin, far_v_twin))
    far_up = move(up3[: HALF + REQUEST], dz=1)
    far_down = move(down3[HALF:], dz=-1)

    key_refs = (own, own_twin, right, right_twin, far_k, far_k_twin, left, left_twin)
    value_refs = (own, own_twin, right, right_twin, far_v, far_v_twin, left, left_twin)
    mean_k = jnp.concatenate([r[TOKENS : TOKENS + BLOCKS] for r in key_refs], axis=0)
    mean_v = jnp.concatenate([r[TOKENS + BLOCKS : split] for r in key_refs], axis=0)
    attend = functools.partial(part, position)
    shared = (mean_k, mean_v, key_refs, value_refs)
    both = (0, HALF + REQUEST)

    up_in, down_in = attend(
        ids_of(far_up),
        *shared,
        (far_up, far_down),
        (((0,), 0, BLOCKS // 2, 0), ((REQUEST,), BLOCKS // 2, BLOCKS // 2, 0)),
    )
    up_in, down_in = move(up_in, dz=-1), move(down_in, dz=1)
    for up, down in ((up3, down3), (up2, down2), (up1, down1)):
        up_part, down_part = attend(
            jnp.concatenate((ids_of(up), ids_of(down))),
            *shared,
            (up, down),
            ((both, 0, BLOCKS, 0), (both, 0, BLOCKS, 1)),
        )
        up_sum, down_sum = merge(up_part, up_in, down_part, down_in)
        up_in, down_in = move(up_sum, dz=-1), move(down_sum, dz=1)
    (own_part,) = attend(ids_of(pay), *shared, (pay,), ((both, 0, BLOCKS, 0),))
    return last(own_part, up_in, down_in)


def solution(mesh):
    placed = (P("ctx", "head"), P("ctx", "head"), P("ctx", "head"), P("ctx", None), P("ctx"))
    return jax.shard_map(
        body, mesh=mesh, in_specs=placed, out_specs=P("ctx", "head"), check_vma=False
    )
```

```python
import functools
import math

import jax
import jax.numpy as jnp
from jax import lax
from jax.experimental import pallas as pl
from jax.experimental.pallas import tpu as pltpu
from jax.sharding import PartitionSpec as P

HD = 128
BLOCK = 32
NX, NZ, NC = 4, 8, 2
BLOCKS = 8
SLOTS = 4
TOKENS = BLOCKS * BLOCK
HALF = TOKENS // 2
REQUEST = 16
STATS = 32
MEANS = 16
PLANE = NX * NC
MOST = 2 * PLANE
FIRST = 2
CHUNK = 4
NEGATIVE = -1e30
ROWS_ROWS = (((1,), (1,)), ((), ()))
COLS_COLS = (((0,), (0,)), ((), ()))
PARAMS = pltpu.CompilerParams(vmem_limit_bytes=24 * 1024 * 1024)


def move(array, dx=0, dz=0, dc=0):
    pairs = []
    for x in range(NX):
        for z in range(NZ):
            for c in range(NC):
                to = (((x + dx) % NX) * NZ + (z + dz) % NZ) * NC + (c ^ dc)
                pairs.append(((x * NZ + z) * NC + c, to))
    return lax.ppermute(array, "ctx", pairs)


def iota(shape, axis):
    return lax.broadcasted_iota(jnp.int32, shape, axis)


def part_kernel(heads, groups, pos_ref, *rest):
    count = len(groups)
    q_refs, rest = rest[:count], rest[count:]
    key_refs, rest = rest[:PLANE], rest[PLANE:]
    value_refs, rest = rest[:PLANE], rest[PLANE:]
    out_refs, rest = rest[:count], rest[count:]
    bufs, rest = rest[:count], rest[count:]
    accs, rest = rest[:count], rest[count:]
    tops, rest = rest[:count], rest[count:]
    sums, rest = rest[:count], rest[count:]
    biases, rest = rest[:count], rest[count:]
    means, ids_vmem, ids_ref, slot_b, slot_k, k_sem, v_sem, mean_sem, ids_sem = rest
    mx, mz, mc = pos_ref[0], pos_ref[1], pos_ref[2]
    inv_root = 1.0 / math.sqrt(HD)

    def copies(g, i, within, n):
        first = pl.multiple_of(within * BLOCK, BLOCK)
        value_first = value_refs[i].shape[0] - TOKENS + first
        return (
            pltpu.make_async_copy(
                key_refs[i].at[pl.ds(first, BLOCK)], bufs[g].at[n, pl.ds(0, BLOCK)], k_sem.at[g, n]
            ),
            pltpu.make_async_copy(
                value_refs[i].at[pl.ds(pl.multiple_of(value_first, 16), BLOCK)],
                bufs[g].at[n, pl.ds(BLOCK, BLOCK)],
                v_sem.at[g, n],
            ),
        )

    ids_copies = []
    for g, (_, _, _, place) in enumerate(groups):
        asked = q_refs[g][place : place + REQUEST, :HD].astype(jnp.float32)
        ids_vmem[g] = asked[:BLOCKS].astype(jnp.int32)
        ids_copies.append(pltpu.make_async_copy(ids_vmem.at[g], ids_ref.at[g], ids_sem.at[g]))
        ids_copies[g].start()
    mean_copies = []
    for i in range(PLANE):
        source = key_refs[i].at[pl.ds(TOKENS, MEANS)]
        mean_copies.append(pltpu.make_async_copy(source, means.at[i], mean_sem.at[i]))
        mean_copies[i].start()
    for copy in ids_copies:
        copy.wait()

    useds = []
    for g, (_, low, blocks, _) in enumerate(groups):

        def ask(b, n, g=g):
            limit = ids_ref[g, b, 2 * SLOTS]
            for p in range(SLOTS):
                owner = ids_ref[g, b, p]
                here = (p < limit) & (((owner >> 1) & (NZ - 1)) == mz)

                @pl.when(here)
                def _(n=n, p=p, owner=owner):
                    within = ids_ref[g, b, SLOTS + p]
                    rel = (((owner >> 4) - mx) & (NX - 1)) * NC + ((owner & 1) ^ mc)
                    slot_b[g, n] = b
                    slot_k[g, n] = rel * BLOCKS + within
                    for i in range(PLANE):

                        @pl.when(rel == i)
                        def _(i=i):
                            for copy in copies(g, i, within, n):
                                copy.start()

                n = n + here.astype(jnp.int32)
            return n

        useds.append(lax.fori_loop(low, low + blocks, ask, jnp.int32(0)))

    def arrived(g, n):
        @pl.when(n < useds[g])
        def _():
            for copy in copies(g, 0, 0, n):
                copy.wait()

    def q_of(g, cols):
        pieces = [q_refs[g][row : row + HALF, cols] for row in groups[g][0]]
        return pieces[0] if len(pieces) == 1 else jnp.concatenate(pieces, axis=0)

    chunks = []
    for g, (_, low, blocks, _) in enumerate(groups):
        tokens = blocks * BLOCK
        used = useds[g]
        chunks.append((jnp.maximum(used - FIRST, 0) + CHUNK - 1) // CHUNK)

        def blank(n, carry, g=g):
            slot_b[g, n] = -1
            bufs[g][n] = jnp.zeros(bufs[g].shape[1:], bufs[g].dtype)
            return carry

        lax.fori_loop(used, FIRST + CHUNK * chunks[g], blank, 0)
        shape = (PLANE * BLOCKS, tokens)
        key_ids, token_blocks = iota(shape, 0), iota(shape, 1) // BLOCK + low

        def exclude(n, table, g=g, key_ids=key_ids, token_blocks=token_blocks):
            hit = (key_ids == slot_k[g, n]) & (token_blocks == slot_b[g, n])
            return jnp.where(hit, NEGATIVE, table)

        bias = jnp.full(shape, math.log(BLOCK), jnp.float32)
        biases[g][...] = lax.fori_loop(0, used, exclude, bias)

    def slot_bias(g, n):
        _, low, blocks, _ = groups[g]
        token_blocks = iota((1, blocks * BLOCK), 1) // BLOCK + low
        return jnp.where(token_blocks == slot_b[g, n], 0.0, NEGATIVE)

    for copy in mean_copies:
        copy.wait()
    mean_tiles = []
    for h in range(heads):
        tiles = [means[i, :, pl.ds(h * HD, HD)].astype(jnp.float32) for i in range(PLANE)]
        both = [[t[:BLOCKS] for t in tiles], [t[BLOCKS:] for t in tiles]]
        mean_tiles.append([jnp.concatenate(b, axis=0).astype(jnp.bfloat16) for b in both])

    for g in range(count):
        for j in range(FIRST):
            arrived(g, j)
        slot_rows = [slot_bias(g, j) for j in range(FIRST)]
        tokens = groups[g][2] * BLOCK
        for h in range(heads):
            cols = pl.ds(h * HD, HD)
            keys = [mean_tiles[h][0]] + [bufs[g][j, :BLOCK, cols] for j in range(FIRST)]
            values = [mean_tiles[h][1]] + [bufs[g][j, BLOCK:, cols] for j in range(FIRST)]
            logits = lax.dot_general(
                jnp.concatenate(keys, axis=0),
                q_of(g, cols),
                ROWS_ROWS,
                preferred_element_type=jnp.float32,
            )
            logits = logits * inv_root
            first = PLANE * BLOCKS
            pieces = [logits[:first] + biases[g][...]]
            for j in range(FIRST):
                pieces.append(logits[first + j * BLOCK : first + (j + 1) * BLOCK] + slot_rows[j])
            logits = jnp.concatenate(pieces, axis=0)
            top = jnp.max(logits, axis=0, keepdims=True)
            weights = jnp.exp(logits - top)
            tops[g][h : h + 1] = top
            sums[g][h : h + 1] = jnp.sum(weights, axis=0, keepdims=True)
            accs[g][cols] = lax.dot_general(
                jnp.concatenate(values, axis=0),
                weights.astype(jnp.bfloat16),
                COLS_COLS,
                preferred_element_type=jnp.float32,
            )

    for g in range(count):

        def chunk(ci, carry, g=g):
            first = FIRST + ci * CHUNK
            for j in range(CHUNK):
                arrived(g, first + j)
            slot_rows = [slot_bias(g, first + j) for j in range(CHUNK)]
            for h in range(heads):
                cols = pl.ds(h * HD, HD)
                keys = [bufs[g][first + j, :BLOCK, cols] for j in range(CHUNK)]
                values = [bufs[g][first + j, BLOCK:, cols] for j in range(CHUNK)]
                logits = lax.dot_general(
                    jnp.concatenate(keys, axis=0),
                    q_of(g, cols),
                    ROWS_ROWS,
                    preferred_element_type=jnp.float32,
                )
                logits = logits * inv_root
                pieces = [
                    logits[j * BLOCK : (j + 1) * BLOCK] + slot_rows[j] for j in range(CHUNK)
                ]
                logits = jnp.concatenate(pieces, axis=0)
                before = tops[g][h : h + 1]
                top = jnp.maximum(before, jnp.max(logits, axis=0, keepdims=True))
                weights = jnp.exp(logits - top)
                ratio = jnp.exp(before - top)
                tops[g][h : h + 1] = top
                sums[g][h : h + 1] = sums[g][h : h + 1] * ratio + jnp.sum(
                    weights, axis=0, keepdims=True
                )
                accs[g][cols] = accs[g][cols] * ratio + lax.dot_general(
                    jnp.concatenate(values, axis=0),
                    weights.astype(jnp.bfloat16),
                    COLS_COLS,
                    preferred_element_type=jnp.float32,
                )
            return carry

        lax.fori_loop(0, chunks[g], chunk, 0)

    for g in range(count):
        top = tops[g][...]
        sent = top.astype(jnp.bfloat16).astype(jnp.float32)
        factor = jnp.exp(top - sent)
        for h in range(heads):
            cols = pl.ds(h * HD, HD)
            out_refs[g][cols] = (accs[g][cols] * factor[h : h + 1]).astype(jnp.bfloat16)
        write_stats(out_refs[g], slice(None), heads, sent, sums[g][...] * factor)


def write_stats(out_ref, lanes, heads, top, total):
    high = total.astype(jnp.bfloat16).astype(jnp.float32)
    rows = (top, high, total - high, jnp.zeros_like(top))
    valid = iota(top.shape, 0) < heads
    rows = [jnp.where(valid, r, 0.0) for r in rows]
    out_ref[heads * HD :, lanes] = jnp.concatenate(rows, axis=0).astype(jnp.bfloat16)


def part(position, key_refs, value_refs, queries, groups):
    columns = queries[0].shape[1]
    heads = columns // HD
    wanted = FIRST + MOST
    vmem = pl.BlockSpec(memory_space=pltpu.VMEM)
    smem = pl.BlockSpec(memory_space=pltpu.SMEM)
    hbm = pl.BlockSpec(memory_space=pltpu.HBM)
    widths = [group[2] * BLOCK for group in groups]
    count = len(groups)
    scratch = [pltpu.VMEM((wanted, 2 * BLOCK, columns), jnp.bfloat16)] * count
    scratch += [pltpu.VMEM((columns, w), jnp.float32) for w in widths]
    scratch += [pltpu.VMEM((8, w), jnp.float32) for w in widths] * 2
    scratch += [pltpu.VMEM((PLANE * BLOCKS, w), jnp.float32) for w in widths]
    scratch += [
        pltpu.VMEM((PLANE, MEANS, columns), jnp.bfloat16),
        pltpu.VMEM((count, BLOCKS, HD), jnp.int32),
        pltpu.SMEM((count, BLOCKS, HD), jnp.int32),
    ]
    scratch += [pltpu.SMEM((count, wanted), jnp.int32)] * 2
    scratch += [pltpu.SemaphoreType.DMA((count, wanted))] * 2
    scratch += [pltpu.SemaphoreType.DMA((PLANE,)), pltpu.SemaphoreType.DMA((count,))]
    return pl.pallas_call(
        functools.partial(part_kernel, heads, groups),
        in_specs=[smem] + [vmem] * count + [hbm] * (2 * PLANE),
        out_specs=[vmem] * count,
        out_shape=[jax.ShapeDtypeStruct((columns + STATS, w), jnp.bfloat16) for w in widths],
        scratch_shapes=scratch,
        compiler_params=PARAMS,
        cost_estimate=pl.CostEstimate(
            flops=4 * 512 * 1024 * columns, bytes_accessed=4 * 1024 * 1024, transcendentals=500000
        ),
    )(position, *queries, *key_refs, *value_refs)


def stats_of(ref, lanes, heads):
    rows = ref[heads * HD :, lanes].astype(jnp.float32)
    return rows[:8], rows[8:16] + rows[16:24]


def merged(heads, parts):
    stats = [stats_of(ref, lanes, heads) for ref, lanes in parts]
    top = functools.reduce(jnp.maximum, [s[0] for s in stats])
    ratios = [jnp.exp(s[0] - top) for s in stats]
    total = functools.reduce(jnp.add, [r * s[1] for r, s in zip(ratios, stats)])
    return top, ratios, total


def merge_kernel(heads, up_ref, up_in_ref, down_ref, down_in_ref, up_out, down_out):
    for own, came, out, up in (
        (up_ref, up_in_ref, up_out, True),
        (down_ref, down_in_ref, down_out, False),
    ):
        width = came.shape[1]
        if width == own.shape[1]:
            lanes = slice(None)
        else:
            lanes = slice(0, width) if up else slice(width, 2 * width)
            rest = slice(width, 2 * width) if up else slice(0, width)
            out[:, rest] = own[:, rest]
        top, ratios, total = merged(heads, ((own, lanes), (came, slice(None))))
        for h in range(heads):
            cols = pl.ds(h * HD, HD)
            one = own[cols, lanes].astype(jnp.float32) * ratios[0][h : h + 1]
            two = came[cols, :].astype(jnp.float32) * ratios[1][h : h + 1]
            out[cols, lanes] = (one + two).astype(jnp.bfloat16)
        write_stats(out, lanes, heads, top, total)


def merge(up, up_in, down, down_in):
    heads = (up.shape[0] - STATS) // HD
    whole = jax.ShapeDtypeStruct(up.shape, jnp.bfloat16)
    return pl.pallas_call(
        functools.partial(merge_kernel, heads),
        out_shape=(whole, whole),
        compiler_params=PARAMS,
        cost_estimate=pl.CostEstimate(
            flops=1000000, bytes_accessed=2 * 1024 * 1024, transcendentals=1000
        ),
    )(up, up_in, down, down_in)


def last_kernel(heads, own_ref, up_ref, down_ref, out_ref):
    refs = (own_ref, up_ref, down_ref)
    _, ratios, total = merged(heads, [(ref, slice(None)) for ref in refs])
    valid = iota(total.shape, 0) < heads
    scales = [r / jnp.where(valid, total, 1.0) for r in ratios]
    for h in range(heads):
        cols = pl.ds(h * HD, HD)
        whole = jnp.zeros((HD, TOKENS), jnp.float32)
        for ref, scale in zip(refs, scales):
            whole = whole + ref[cols].astype(jnp.float32) * scale[h : h + 1]
        out_ref[:, cols] = jnp.transpose(whole).astype(out_ref.dtype)


def last(own, up, down):
    columns = own.shape[0] - STATS
    return pl.pallas_call(
        functools.partial(last_kernel, columns // HD),
        out_shape=jax.ShapeDtypeStruct((TOKENS, columns), jnp.bfloat16),
        compiler_params=PARAMS,
    )(own, up, down)


def body(queries, key_tokens, value_tokens, pair_keys, pair_count):
    tok_rows, columns = queries.shape
    assert lax.axis_size("ctx") == NX * NZ * NC
    assert tok_rows == TOKENS and pair_keys.shape == (BLOCKS, SLOTS)
    me = lax.axis_index("ctx")
    position = jnp.stack((me // (NZ * NC), (me // NC) % NZ, me % NC)).astype(jnp.int32)
    barrier = lax.optimization_barrier

    asked = jnp.concatenate(
        (pair_keys // BLOCKS, pair_keys % BLOCKS, pair_count[:, None]), axis=1
    ).astype(jnp.bfloat16)
    asked = jnp.pad(asked, ((0, REQUEST - BLOCKS), (0, columns - 2 * SLOTS - 1)))
    pay = jnp.concatenate((queries[:HALF], asked, queries[HALF:]), axis=0)

    def means(tokens):
        grouped = tokens.reshape(BLOCKS, BLOCK, columns).astype(jnp.float32)
        return jnp.mean(grouped, axis=1).astype(jnp.bfloat16)

    split = TOKENS + MEANS
    own = jnp.concatenate(
        (key_tokens, means(key_tokens), means(value_tokens), value_tokens), axis=0
    )
    pay, own = barrier((pay, own))
    up1, down1 = move(pay, dz=1), move(pay, dz=-1)
    left, right = move(own, dx=1), move(own, dx=-1)
    own_twin = move(own, dc=1)
    up1, down1, left, right, own_twin = barrier((up1, down1, left, right, own_twin))

    up2, down2 = move(up1, dz=1), move(down1, dz=-1)
    far_k, far_v = move(left[:split], dx=1), move(right[split:], dx=-1)
    left_twin = move(left, dc=1)
    up2, down2, far_k, far_v, left_twin = barrier((up2, down2, far_k, far_v, left_twin))

    up3, down3 = move(up2, dz=1), move(down2, dz=-1)
    right_twin, far_k_twin, far_v_twin = move(right, dc=1), move(far_k, dc=1), move(far_v, dc=1)
    up3, down3, right_twin, far_k_twin, far_v_twin = barrier(
        (up3, down3, right_twin, far_k_twin, far_v_twin)
    )
    far_up = move(up3[: HALF + REQUEST], dz=1)
    far_down = move(down3[HALF:], dz=-1)

    key_refs = (own, own_twin, right, right_twin, far_k, far_k_twin, left, left_twin)
    value_refs = (own, own_twin, right, right_twin, far_v, far_v_twin, left, left_twin)
    attend = functools.partial(part, position, key_refs, value_refs)
    both, last_half = (0, HALF + REQUEST), BLOCKS // 2

    up_in, down_in = attend(
        (far_up, far_down), (((0,), 0, last_half, HALF), ((REQUEST,), last_half, last_half, 0))
    )
    up_in, down_in = move(up_in, dz=-1), move(down_in, dz=1)
    for up, down in ((up3, down3), (up2, down2), (up1, down1)):
        up_part, down_part = attend((up, down), ((both, 0, BLOCKS, HALF),) * 2)
        up_sum, down_sum = merge(up_part, up_in, down_part, down_in)
        up_in, down_in = move(up_sum, dz=-1), move(down_sum, dz=1)
    (own_part,) = attend((pay,), ((both, 0, BLOCKS, HALF),))
    return last(own_part, up_in, down_in)


def solution(mesh):
    placed = (P("ctx", "head"), P("ctx", "head"), P("ctx", "head"), P("ctx", None), P("ctx"))
    return jax.shard_map(
        body, mesh=mesh, in_specs=placed, out_specs=P("ctx", "head"), check_vma=False
    )
```

```python
import functools
import math

import jax
import jax.numpy as jnp
from jax import lax
from jax.experimental import pallas as pl
from jax.experimental.pallas import tpu as pltpu
from jax.sharding import PartitionSpec as P

HD = 128
BLOCK = 32
NX, NZ, NC = 4, 8, 2
BLOCKS = 8
SLOTS = 4
TOKENS = BLOCKS * BLOCK
HALF = TOKENS // 2
REQUEST = 16
STATS = 32
MEANS = 16
PLANE = NX * NC
MOST = 2 * PLANE
FIRST = 2
CHUNK = 4
NEGATIVE = -1e30
ROWS_ROWS = (((1,), (1,)), ((), ()))
COLS_COLS = (((0,), (0,)), ((), ()))
PARAMS = pltpu.CompilerParams(vmem_limit_bytes=24 * 1024 * 1024)


def move(array, dx=0, dz=0, dc=0):
    pairs = []
    for x in range(NX):
        for z in range(NZ):
            for c in range(NC):
                to = (((x + dx) % NX) * NZ + (z + dz) % NZ) * NC + (c ^ dc)
                pairs.append(((x * NZ + z) * NC + c, to))
    return lax.ppermute(array, "ctx", pairs)


def iota(shape, axis):
    return lax.broadcasted_iota(jnp.int32, shape, axis)


def part_kernel(heads, groups, pos_ref, *rest):
    count = len(groups)
    q_refs, rest = rest[:count], rest[count:]
    key_refs, rest = rest[:PLANE], rest[PLANE:]
    value_refs, rest = rest[:PLANE], rest[PLANE:]
    out_refs, rest = rest[:count], rest[count:]
    bufs, rest = rest[:count], rest[count:]
    accs, rest = rest[:count], rest[count:]
    tops, rest = rest[:count], rest[count:]
    sums, rest = rest[:count], rest[count:]
    biases, rest = rest[:count], rest[count:]
    means, ids_vmem, ids_ref, slot_b, slot_k, k_sem, v_sem, mean_sem, ids_sem = rest
    mx, mz, mc = pos_ref[0], pos_ref[1], pos_ref[2]
    inv_root = 1.0 / math.sqrt(HD)

    def copies(g, i, within, n):
        first = pl.multiple_of(within * BLOCK, BLOCK)
        value_first = value_refs[i].shape[0] - TOKENS + first
        return (
            pltpu.make_async_copy(
                key_refs[i].at[pl.ds(first, BLOCK)], bufs[g].at[n, pl.ds(0, BLOCK)], k_sem.at[g, n]
            ),
            pltpu.make_async_copy(
                value_refs[i].at[pl.ds(pl.multiple_of(value_first, 16), BLOCK)],
                bufs[g].at[n, pl.ds(BLOCK, BLOCK)],
                v_sem.at[g, n],
            ),
        )

    ids_copies = []
    for g, (_, _, _, place) in enumerate(groups):
        asked = q_refs[g][place : place + REQUEST, :HD].astype(jnp.float32)
        ids_vmem[g] = asked[:BLOCKS].astype(jnp.int32)
        ids_copies.append(pltpu.make_async_copy(ids_vmem.at[g], ids_ref.at[g], ids_sem.at[g]))
        ids_copies[g].start()
    mean_copies = []
    for i in range(PLANE):
        source = key_refs[i].at[pl.ds(TOKENS, MEANS)]
        mean_copies.append(pltpu.make_async_copy(source, means.at[i], mean_sem.at[i]))
        mean_copies[i].start()
    for copy in ids_copies:
        copy.wait()

    useds = []
    for g, (_, low, blocks, _) in enumerate(groups):

        def ask(b, n, g=g):
            limit = ids_ref[g, b, 2 * SLOTS]
            for p in range(SLOTS):
                owner = ids_ref[g, b, p]
                here = (p < limit) & (((owner >> 1) & (NZ - 1)) == mz)

                @pl.when(here)
                def _(n=n, p=p, owner=owner):
                    within = ids_ref[g, b, SLOTS + p]
                    rel = (((owner >> 4) - mx) & (NX - 1)) * NC + ((owner & 1) ^ mc)
                    slot_b[g, n] = b
                    slot_k[g, n] = rel * BLOCKS + within
                    for i in range(PLANE):

                        @pl.when(rel == i)
                        def _(i=i):
                            for copy in copies(g, i, within, n):
                                copy.start()

                n = n + here.astype(jnp.int32)
            return n

        useds.append(lax.fori_loop(low, low + blocks, ask, jnp.int32(0)))

    def arrived(g, n):
        @pl.when(n < useds[g])
        def _():
            for copy in copies(g, 0, 0, n):
                copy.wait()

    def q_of(g, cols):
        pieces = [q_refs[g][row : row + HALF, cols] for row in groups[g][0]]
        return pieces[0] if len(pieces) == 1 else jnp.concatenate(pieces, axis=0)

    chunks = []
    for g, (_, low, blocks, _) in enumerate(groups):
        tokens = blocks * BLOCK
        used = useds[g]
        chunks.append((jnp.maximum(used - FIRST, 0) + CHUNK - 1) // CHUNK)

        def blank(n, carry, g=g):
            slot_b[g, n] = -1
            bufs[g][n] = jnp.zeros(bufs[g].shape[1:], bufs[g].dtype)
            return carry

        lax.fori_loop(used, FIRST + CHUNK * chunks[g], blank, 0)
        shape = (PLANE * BLOCKS, tokens)
        key_ids, token_blocks = iota(shape, 0), iota(shape, 1) // BLOCK + low

        def exclude(n, table, g=g, key_ids=key_ids, token_blocks=token_blocks):
            hit = (key_ids == slot_k[g, n]) & (token_blocks == slot_b[g, n])
            return jnp.where(hit, NEGATIVE, table)

        bias = jnp.full(shape, math.log(BLOCK), jnp.float32)
        biases[g][...] = lax.fori_loop(0, used, exclude, bias)

    def slot_bias(g, n):
        _, low, blocks, _ = groups[g]
        token_blocks = iota((1, blocks * BLOCK), 1) // BLOCK + low
        return jnp.where(token_blocks == slot_b[g, n], 0.0, NEGATIVE)

    for copy in mean_copies:
        copy.wait()
    mean_tiles = []
    for h in range(heads):
        tiles = [means[i, :, pl.ds(h * HD, HD)].astype(jnp.float32) for i in range(PLANE)]
        both = [[t[:BLOCKS] for t in tiles], [t[BLOCKS:] for t in tiles]]
        mean_tiles.append([jnp.concatenate(b, axis=0).astype(jnp.bfloat16) for b in both])

    for g in range(count):
        for j in range(FIRST):
            arrived(g, j)
        slot_rows = [slot_bias(g, j) for j in range(FIRST)]
        tokens = groups[g][2] * BLOCK
        for h in range(heads):
            cols = pl.ds(h * HD, HD)
            keys = [mean_tiles[h][0]] + [bufs[g][j, :BLOCK, cols] for j in range(FIRST)]
            values = [mean_tiles[h][1]] + [bufs[g][j, BLOCK:, cols] for j in range(FIRST)]
            logits = lax.dot_general(
                jnp.concatenate(keys, axis=0),
                q_of(g, cols),
                ROWS_ROWS,
                preferred_element_type=jnp.float32,
            )
            logits = logits * inv_root
            first = PLANE * BLOCKS
            pieces = [logits[:first] + biases[g][...]]
            for j in range(FIRST):
                pieces.append(logits[first + j * BLOCK : first + (j + 1) * BLOCK] + slot_rows[j])
            logits = jnp.concatenate(pieces, axis=0)
            top = jnp.max(logits, axis=0, keepdims=True)
            weights = jnp.exp(logits - top)
            tops[g][h : h + 1] = top
            sums[g][h : h + 1] = jnp.sum(weights, axis=0, keepdims=True)
            accs[g][cols] = lax.dot_general(
                jnp.concatenate(values, axis=0),
                weights.astype(jnp.bfloat16),
                COLS_COLS,
                preferred_element_type=jnp.float32,
            )

    for g in range(count):

        def chunk(ci, carry, g=g):
            first = FIRST + ci * CHUNK
            for j in range(CHUNK):
                arrived(g, first + j)
            slot_rows = [slot_bias(g, first + j) for j in range(CHUNK)]
            for h in range(heads):
                cols = pl.ds(h * HD, HD)
                keys = [bufs[g][first + j, :BLOCK, cols] for j in range(CHUNK)]
                values = [bufs[g][first + j, BLOCK:, cols] for j in range(CHUNK)]
                logits = lax.dot_general(
                    jnp.concatenate(keys, axis=0),
                    q_of(g, cols),
                    ROWS_ROWS,
                    preferred_element_type=jnp.float32,
                )
                logits = logits * inv_root
                pieces = [
                    logits[j * BLOCK : (j + 1) * BLOCK] + slot_rows[j] for j in range(CHUNK)
                ]
                logits = jnp.concatenate(pieces, axis=0)
                before = tops[g][h : h + 1]
                top = jnp.maximum(before, jnp.max(logits, axis=0, keepdims=True))
                weights = jnp.exp(logits - top)
                ratio = jnp.exp(before - top)
                tops[g][h : h + 1] = top
                sums[g][h : h + 1] = sums[g][h : h + 1] * ratio + jnp.sum(
                    weights, axis=0, keepdims=True
                )
                accs[g][cols] = accs[g][cols] * ratio + lax.dot_general(
                    jnp.concatenate(values, axis=0),
                    weights.astype(jnp.bfloat16),
                    COLS_COLS,
                    preferred_element_type=jnp.float32,
                )
            return carry

        lax.fori_loop(0, chunks[g], chunk, 0)

    for g in range(count):
        top = tops[g][...]
        sent = top.astype(jnp.bfloat16).astype(jnp.float32)
        factor = jnp.exp(top - sent)
        for h in range(heads):
            cols = pl.ds(h * HD, HD)
            out_refs[g][cols] = (accs[g][cols] * factor[h : h + 1]).astype(jnp.bfloat16)
        write_stats(out_refs[g], slice(None), heads, sent, sums[g][...] * factor)


def write_stats(out_ref, lanes, heads, top, total):
    high = total.astype(jnp.bfloat16).astype(jnp.float32)
    rows = (top, high, total - high, jnp.zeros_like(top))
    valid = iota(top.shape, 0) < heads
    rows = [jnp.where(valid, r, 0.0) for r in rows]
    out_ref[heads * HD :, lanes] = jnp.concatenate(rows, axis=0).astype(jnp.bfloat16)


def part(position, key_refs, value_refs, queries, groups):
    columns = queries[0].shape[1]
    heads = columns // HD
    wanted = FIRST + MOST
    vmem = pl.BlockSpec(memory_space=pltpu.VMEM)
    smem = pl.BlockSpec(memory_space=pltpu.SMEM)
    widths = [group[2] * BLOCK for group in groups]
    count = len(groups)
    scratch = [pltpu.VMEM((wanted, 2 * BLOCK, columns), jnp.bfloat16)] * count
    scratch += [pltpu.VMEM((columns, w), jnp.float32) for w in widths]
    scratch += [pltpu.VMEM((8, w), jnp.float32) for w in widths] * 2
    scratch += [pltpu.VMEM((PLANE * BLOCKS, w), jnp.float32) for w in widths]
    scratch += [
        pltpu.VMEM((PLANE, MEANS, columns), jnp.bfloat16),
        pltpu.VMEM((count, BLOCKS, HD), jnp.int32),
        pltpu.SMEM((count, BLOCKS, HD), jnp.int32),
    ]
    scratch += [pltpu.SMEM((count, wanted), jnp.int32)] * 2
    scratch += [pltpu.SemaphoreType.DMA((count, wanted))] * 2
    scratch += [pltpu.SemaphoreType.DMA((PLANE,)), pltpu.SemaphoreType.DMA((count,))]
    return pl.pallas_call(
        functools.partial(part_kernel, heads, groups),
        in_specs=[smem] + [vmem] * (count + 2 * PLANE),
        out_specs=[vmem] * count,
        out_shape=[jax.ShapeDtypeStruct((columns + STATS, w), jnp.bfloat16) for w in widths],
        scratch_shapes=scratch,
        compiler_params=PARAMS,
        cost_estimate=pl.CostEstimate(
            flops=4 * 512 * 1024 * columns, bytes_accessed=4 * 1024 * 1024, transcendentals=500000
        ),
    )(position, *queries, *key_refs, *value_refs)


def stats_of(ref, lanes, heads):
    rows = ref[heads * HD :, lanes].astype(jnp.float32)
    return rows[:8], rows[8:16] + rows[16:24]


def merged(heads, parts):
    stats = [stats_of(ref, lanes, heads) for ref, lanes in parts]
    top = functools.reduce(jnp.maximum, [s[0] for s in stats])
    ratios = [jnp.exp(s[0] - top) for s in stats]
    total = functools.reduce(jnp.add, [r * s[1] for r, s in zip(ratios, stats)])
    return top, ratios, total


def merge_kernel(heads, up_ref, up_in_ref, down_ref, down_in_ref, up_out, down_out):
    for own, came, out, up in (
        (up_ref, up_in_ref, up_out, True),
        (down_ref, down_in_ref, down_out, False),
    ):
        width = came.shape[1]
        if width == own.shape[1]:
            lanes = slice(None)
        else:
            lanes = slice(0, width) if up else slice(width, 2 * width)
            rest = slice(width, 2 * width) if up else slice(0, width)
            out[:, rest] = own[:, rest]
        top, ratios, total = merged(heads, ((own, lanes), (came, slice(None))))
        for h in range(heads):
            cols = pl.ds(h * HD, HD)
            one = own[cols, lanes].astype(jnp.float32) * ratios[0][h : h + 1]
            two = came[cols, :].astype(jnp.float32) * ratios[1][h : h + 1]
            out[cols, lanes] = (one + two).astype(jnp.bfloat16)
        write_stats(out, lanes, heads, top, total)


def merge(up, up_in, down, down_in):
    heads = (up.shape[0] - STATS) // HD
    whole = jax.ShapeDtypeStruct(up.shape, jnp.bfloat16)
    return pl.pallas_call(
        functools.partial(merge_kernel, heads),
        out_shape=(whole, whole),
        compiler_params=PARAMS,
        cost_estimate=pl.CostEstimate(
            flops=1000000, bytes_accessed=2 * 1024 * 1024, transcendentals=1000
        ),
    )(up, up_in, down, down_in)


def last_kernel(heads, own_ref, up_ref, down_ref, out_ref):
    refs = (own_ref, up_ref, down_ref)
    _, ratios, total = merged(heads, [(ref, slice(None)) for ref in refs])
    valid = iota(total.shape, 0) < heads
    scales = [r / jnp.where(valid, total, 1.0) for r in ratios]
    for h in range(heads):
        cols = pl.ds(h * HD, HD)
        whole = jnp.zeros((HD, TOKENS), jnp.float32)
        for ref, scale in zip(refs, scales):
            whole = whole + ref[cols].astype(jnp.float32) * scale[h : h + 1]
        out_ref[:, cols] = jnp.transpose(whole).astype(out_ref.dtype)


def last(own, up, down):
    columns = own.shape[0] - STATS
    return pl.pallas_call(
        functools.partial(last_kernel, columns // HD),
        out_shape=jax.ShapeDtypeStruct((TOKENS, columns), jnp.bfloat16),
        compiler_params=PARAMS,
    )(own, up, down)


def body(queries, key_tokens, value_tokens, pair_keys, pair_count):
    tok_rows, columns = queries.shape
    assert lax.axis_size("ctx") == NX * NZ * NC
    assert tok_rows == TOKENS and pair_keys.shape == (BLOCKS, SLOTS)
    me = lax.axis_index("ctx")
    position = jnp.stack((me // (NZ * NC), (me // NC) % NZ, me % NC)).astype(jnp.int32)
    barrier = lax.optimization_barrier

    asked = jnp.concatenate(
        (pair_keys // BLOCKS, pair_keys % BLOCKS, pair_count[:, None]), axis=1
    ).astype(jnp.bfloat16)
    asked = jnp.pad(asked, ((0, REQUEST - BLOCKS), (0, columns - 2 * SLOTS - 1)))
    pay = jnp.concatenate((queries[:HALF], asked, queries[HALF:]), axis=0)

    def means(tokens):
        grouped = tokens.reshape(BLOCKS, BLOCK, columns).astype(jnp.float32)
        return jnp.mean(grouped, axis=1).astype(jnp.bfloat16)

    split = TOKENS + MEANS
    own = jnp.concatenate(
        (key_tokens, means(key_tokens), means(value_tokens), value_tokens), axis=0
    )
    pay, own = barrier((pay, own))
    up1, down1 = move(pay, dz=1), move(pay, dz=-1)
    left, right = move(own, dx=1), move(own, dx=-1)
    own_twin = move(own, dc=1)
    up1, down1, left, right = barrier((up1, down1, left, right))

    up2, down2 = move(up1, dz=1), move(down1, dz=-1)
    far_k, far_v = move(left[:split], dx=1), move(right[split:], dx=-1)
    up2, down2, far_k, far_v, own_twin = barrier((up2, down2, far_k, far_v, own_twin))

    up3, down3 = move(up2, dz=1), move(down2, dz=-1)
    left_twin, right_twin = move(left, dc=1), move(right, dc=1)
    up3, down3, left_twin, right_twin = barrier((up3, down3, left_twin, right_twin))
    far_k_twin, far_v_twin = move(far_k, dc=1), move(far_v, dc=1)
    far_up = move(up3[: HALF + REQUEST], dz=1)
    far_down = move(down3[HALF:], dz=-1)

    key_refs = (own, own_twin, right, right_twin, far_k, far_k_twin, left, left_twin)
    value_refs = (own, own_twin, right, right_twin, far_v, far_v_twin, left, left_twin)
    attend = functools.partial(part, position, key_refs, value_refs)
    both, last_half = (0, HALF + REQUEST), BLOCKS // 2

    up_in, down_in = attend(
        (far_up, far_down), (((0,), 0, last_half, HALF), ((REQUEST,), last_half, last_half, 0))
    )
    up_in, down_in = move(up_in, dz=-1), move(down_in, dz=1)
    for up, down in ((up3, down3), (up2, down2), (up1, down1)):
        up_part, down_part = attend((up, down), ((both, 0, BLOCKS, HALF),) * 2)
        up_sum, down_sum = merge(up_part, up_in, down_part, down_in)
        up_in, down_in = move(up_sum, dz=-1), move(down_sum, dz=1)
    (own_part,) = attend((pay,), ((both, 0, BLOCKS, HALF),))
    return last(own_part, up_in, down_in)


def solution(mesh):
    placed = (P("ctx", "head"), P("ctx", "head"), P("ctx", "head"), P("ctx", None), P("ctx"))
    return jax.shard_map(
        body, mesh=mesh, in_specs=placed, out_specs=P("ctx", "head"), check_vma=False
    )
```

```python
import functools
import math

import jax
import jax.numpy as jnp
from jax import lax
from jax.experimental import pallas as pl
from jax.experimental.pallas import tpu as pltpu
from jax.sharding import PartitionSpec as P

HD = 128
BLOCK = 32
NX, NZ, NC = 4, 8, 2
BLOCKS = 8
SLOTS = 4
TOKENS = BLOCKS * BLOCK
HALF = TOKENS // 2
REQUEST = 16
STATS = 32
MEANS = 16
PLANE = NX * NC
MOST = 2 * PLANE
FIRST = 2
CHUNK = 4
NEGATIVE = -1e30
ROWS_ROWS = (((1,), (1,)), ((), ()))
COLS_COLS = (((0,), (0,)), ((), ()))
PARAMS = pltpu.CompilerParams(vmem_limit_bytes=10 * 1024 * 1024)


def move(array, dx=0, dz=0, dc=0):
    pairs = []
    for x in range(NX):
        for z in range(NZ):
            for c in range(NC):
                to = (((x + dx) % NX) * NZ + (z + dz) % NZ) * NC + (c ^ dc)
                pairs.append(((x * NZ + z) * NC + c, to))
    return lax.ppermute(array, "ctx", pairs)


def iota(shape, axis):
    return lax.broadcasted_iota(jnp.int32, shape, axis)


ENTRY = 32
MEAN_KEYS = PLANE * BLOCKS


def list_kernel(first, spec, pos_ref, asked_ref, bias_ref, list_ref, ids_vmem, ids_ref, sem):
    mx, mz, mc = pos_ref[0], pos_ref[1], pos_ref[2]
    tables = ids_vmem.shape[0]
    row = iota((BLOCKS, HD), 0)
    for table in range(tables):
        rows = pl.ds(first + table * REQUEST, REQUEST)
        request = asked_ref[rows, :HD].astype(jnp.float32)
        owner, within = request[:BLOCKS].astype(jnp.int32), request[BLOCKS:].astype(jnp.int32)
        here = (owner >= 0) & (((owner >> 1) & (NZ - 1)) == mz)
        rel = (((owner >> 4) - mx) & (NX - 1)) * NC + ((owner & 1) ^ mc)
        ids_vmem[table] = jnp.where(here, (row * PLANE + rel) * BLOCKS + within, -1)
    ids_copy = pltpu.make_async_copy(ids_vmem, ids_ref, sem)
    ids_copy.start()
    ids_copy.wait()

    for g, (table, low, high) in enumerate(spec):

        def ask(b, n, g=g, table=table):
            for p in range(SLOTS):
                code = ids_ref[table, b, p]
                list_ref[g, ENTRY + n] = code
                n = n + (code >= 0).astype(jnp.int32)
            return n

        used = lax.fori_loop(low, high, ask, jnp.int32(0))
        list_ref[g, 0] = used

        def blank(n, carry, g=g):
            list_ref[g, ENTRY + n] = -1
            return carry

        lax.fori_loop(used, FIRST + MOST, blank, 0)

    shape = (MEAN_KEYS, TOKENS)
    key_ids, token_blocks = iota(shape, 0), iota(shape, 1) // BLOCK
    for table in range(tables):
        bias = jnp.full(shape, math.log(BLOCK), jnp.float32)
        for g in range(len(spec)):
            if spec[g][0] != table:
                continue

            def exclude(n, bias, g=g):
                code = list_ref[g, ENTRY + n]
                hit = (key_ids == (code & (MEAN_KEYS - 1))) & (token_blocks == code >> 6)
                return jnp.where(hit, NEGATIVE, bias)

            bias = lax.fori_loop(0, list_ref[g, 0], exclude, bias)
        bias_ref[table] = bias


def make_lists(position, asked, first, tables, spec):
    vmem = pl.BlockSpec(memory_space=pltpu.VMEM)
    smem = pl.BlockSpec(memory_space=pltpu.SMEM)
    return pl.pallas_call(
        functools.partial(list_kernel, first, spec),
        in_specs=[smem, vmem],
        out_specs=[vmem, smem],
        out_shape=[
            jax.ShapeDtypeStruct((tables, MEAN_KEYS, TOKENS), jnp.float32),
            jax.ShapeDtypeStruct((len(spec), HD), jnp.int32),
        ],
        scratch_shapes=[
            pltpu.VMEM((tables, BLOCKS, HD), jnp.int32),
            pltpu.SMEM((tables, BLOCKS, HD), jnp.int32),
            pltpu.SemaphoreType.DMA,
        ],
        compiler_params=PARAMS,
        cost_estimate=pl.CostEstimate(flops=1000000, bytes_accessed=1024 * 1024, transcendentals=0),
    )(position, asked)


def means_kernel(*refs):
    sources, (mean_k_ref, mean_v_ref) = refs[:PLANE], refs[PLANE:]
    tiles = [source[TOKENS : TOKENS + MEANS].astype(jnp.float32) for source in sources]
    mean_k_ref[...] = jnp.concatenate([t[:BLOCKS] for t in tiles], axis=0).astype(jnp.bfloat16)
    mean_v_ref[...] = jnp.concatenate([t[BLOCKS:] for t in tiles], axis=0).astype(jnp.bfloat16)


def gather_means(sources):
    shape = jax.ShapeDtypeStruct((MEAN_KEYS, sources[0].shape[1]), jnp.bfloat16)
    return pl.pallas_call(
        means_kernel,
        out_shape=(shape, shape),
        compiler_params=PARAMS,
        cost_estimate=pl.CostEstimate(flops=1000000, bytes_accessed=1024 * 1024, transcendentals=0),
    )(*sources)


def own_kernel(key_ref, value_ref, out_ref, sem):
    split = TOKENS + MEANS
    starts = (0, split)
    copies = []
    for n, ref in enumerate((key_ref, value_ref)):
        target = out_ref.at[pl.ds(starts[n], TOKENS)]
        copies.append(pltpu.make_async_copy(ref, target, sem.at[n]))
        copies[n].start()
    means = []
    for first, copy in zip(starts, copies):
        copy.wait()
        for b in range(BLOCKS):
            rows = pl.ds(first + b * BLOCK, BLOCK)
            block = out_ref[rows].astype(jnp.float32)
            means.append(jnp.sum(block, axis=0, keepdims=True) * (1.0 / BLOCK))
    out_ref[TOKENS:split] = jnp.concatenate(means, axis=0).astype(jnp.bfloat16)


def make_own(keys, values):
    rows = 2 * TOKENS + MEANS
    return pl.pallas_call(
        own_kernel,
        in_specs=[pl.BlockSpec(memory_space=pl.ANY)] * 2,
        out_shape=jax.ShapeDtypeStruct((rows, keys.shape[1]), jnp.bfloat16),
        scratch_shapes=[pltpu.SemaphoreType.DMA((2,))],
        compiler_params=PARAMS,
    )(keys, values)


def part_kernel(heads, groups, list_ref, mean_k_ref, mean_v_ref, bias_ref, *rest):
    count = len(groups)
    key_refs, rest = rest[:PLANE], rest[PLANE:]
    value_refs, rest = rest[:PLANE], rest[PLANE:]
    q_refs, rest = rest[:count], rest[count:]
    out_refs, rest = rest[:count], rest[count:]
    accs, rest = rest[:count], rest[count:]
    tops, rest = rest[:count], rest[count:]
    sums, bufs = rest[:count], rest[count:]
    inv_root = 1.0 / math.sqrt(HD)
    chunks = []
    for g in range(count):
        which = groups[g][3]
        used = list_ref[which, 0]
        chunks.append((jnp.maximum(used - FIRST, 0) + CHUNK - 1) // CHUNK)

        def fetch(n, carry, g=g, which=which):
            key = list_ref[which, ENTRY + n] & (MEAN_KEYS - 1)
            first = pl.multiple_of((key % BLOCKS) * BLOCK, BLOCK)
            for i in range(PLANE):

                @pl.when(key // BLOCKS == i)
                def _(i=i):
                    skip = value_refs[i].shape[0] - TOKENS
                    rows = pl.ds(pl.multiple_of(first + skip, 16), BLOCK)
                    bufs[g][n, :BLOCK] = key_refs[i][pl.ds(first, BLOCK)]
                    bufs[g][n, BLOCK:] = value_refs[i][rows]

            return carry

        lax.fori_loop(0, FIRST + CHUNK * chunks[g], fetch, 0)

    def slots_of(g, first, number):
        _, low, blocks, which, _ = groups[g]
        token_blocks = iota((1, blocks * BLOCK), 1) // BLOCK + low
        places, rows = [], []
        for j in range(number):
            code = list_ref[which, ENTRY + first + j]
            places.append((g, first + j))
            rows.append(jnp.where(token_blocks == code >> 6, 0.0, NEGATIVE))
        return places, rows

    def keys_of(places, cols):
        return [bufs[g][n, :BLOCK, cols] for g, n in places]

    def values_of(places, cols):
        return [bufs[g][n, BLOCK:, cols] for g, n in places]

    def logits_of(g, keys, cols, biases):
        pieces = [q_refs[g][row : row + HALF, cols] for row in groups[g][0]]
        queries = pieces[0] if len(pieces) == 1 else jnp.concatenate(pieces, axis=0)
        logits = lax.dot_general(
            jnp.concatenate(keys, axis=0), queries, ROWS_ROWS, preferred_element_type=jnp.float32
        )
        logits = logits * inv_root
        pieces, row = [], 0
        for key, bias in zip(keys, biases):
            pieces.append(logits[row : row + key.shape[0]] + bias)
            row += key.shape[0]
        return jnp.concatenate(pieces, axis=0)

    def summed(values, weights):
        return lax.dot_general(
            jnp.concatenate(values, axis=0),
            weights,
            COLS_COLS,
            preferred_element_type=jnp.float32,
        )

    all_cols = [pl.ds(h * HD, HD) for h in range(heads)]
    for g in range(count):
        _, low, blocks, _, table = groups[g]
        places, rows = slots_of(g, 0, FIRST)
        bias = bias_ref[table, :, low * BLOCK : (low + blocks) * BLOCK]
        tiles = [
            logits_of(g, [mean_k_ref[:, cols]] + keys_of(places, cols), cols, [bias] + rows)
            for cols in all_cols
        ]
        for h, cols in enumerate(all_cols):
            top = jnp.max(tiles[h], axis=0, keepdims=True)
            weights = jnp.exp(tiles[h] - top)
            tops[g][h : h + 1] = top
            sums[g][h : h + 1] = jnp.sum(weights, axis=0, keepdims=True)
            tiles[h] = weights.astype(jnp.bfloat16)
        for h, cols in enumerate(all_cols):
            accs[g][cols] = summed([mean_v_ref[:, cols]] + values_of(places, cols), tiles[h])

    for g in range(count):

        def chunk(ci, carry, g=g):
            places, rows = slots_of(g, FIRST + ci * CHUNK, CHUNK)
            tiles = [logits_of(g, keys_of(places, cols), cols, rows) for cols in all_cols]
            ratios = []
            for h in range(heads):
                before = tops[g][h : h + 1]
                top = jnp.maximum(before, jnp.max(tiles[h], axis=0, keepdims=True))
                weights = jnp.exp(tiles[h] - top)
                ratio = jnp.exp(before - top)
                tops[g][h : h + 1] = top
                sums[g][h : h + 1] = sums[g][h : h + 1] * ratio + jnp.sum(
                    weights, axis=0, keepdims=True
                )
                tiles[h] = weights.astype(jnp.bfloat16)
                ratios.append(ratio)
            for h, cols in enumerate(all_cols):
                accs[g][cols] = accs[g][cols] * ratios[h] + summed(
                    values_of(places, cols), tiles[h]
                )
            return carry

        lax.fori_loop(0, chunks[g], chunk, 0)

    for g in range(count):
        top = tops[g][...]
        sent = top.astype(jnp.bfloat16).astype(jnp.float32)
        factor = jnp.exp(top - sent)
        for h, cols in enumerate(all_cols):
            out_refs[g][cols] = (accs[g][cols] * factor[h : h + 1]).astype(jnp.bfloat16)
        write_stats(out_refs[g], slice(None), heads, sent, sums[g][...] * factor)


def write_stats(out_ref, lanes, heads, top, total):
    high = total.astype(jnp.bfloat16).astype(jnp.float32)
    rows = (top, high, total - high, jnp.zeros_like(top))
    valid = iota(top.shape, 0) < heads
    rows = [jnp.where(valid, r, 0.0) for r in rows]
    out_ref[heads * HD :, lanes] = jnp.concatenate(rows, axis=0).astype(jnp.bfloat16)


def part(plane, bias, lists, queries, groups):
    columns = queries[0].shape[1]
    heads = columns // HD
    vmem = pl.BlockSpec(memory_space=pltpu.VMEM)
    smem = pl.BlockSpec(memory_space=pltpu.SMEM)
    widths = [group[2] * BLOCK for group in groups]
    scratch = [pltpu.VMEM((columns, w), jnp.float32) for w in widths]
    scratch += [pltpu.VMEM((8, w), jnp.float32) for w in widths] * 2
    scratch += [pltpu.VMEM((FIRST + MOST, 2 * BLOCK, columns), jnp.bfloat16) for _ in widths]
    mean_k, mean_v, key_refs, value_refs = plane
    operands = (mean_k, mean_v, bias, *key_refs, *value_refs, *queries)
    return pl.pallas_call(
        functools.partial(part_kernel, heads, groups),
        in_specs=[smem] + [vmem] * len(operands),
        out_specs=[vmem] * len(groups),
        out_shape=[jax.ShapeDtypeStruct((columns + STATS, w), jnp.bfloat16) for w in widths],
        scratch_shapes=scratch,
        compiler_params=PARAMS,
        cost_estimate=pl.CostEstimate(
            flops=4 * 512 * 1024 * columns, bytes_accessed=4 * 1024 * 1024, transcendentals=500000
        ),
    )(lists, *operands)


def stats_of(ref, lanes, heads):
    rows = ref[heads * HD :, lanes].astype(jnp.float32)
    return rows[:8], rows[8:16] + rows[16:24]


def merged(heads, parts):
    stats = [stats_of(ref, lanes, heads) for ref, lanes in parts]
    top = functools.reduce(jnp.maximum, [s[0] for s in stats])
    ratios = [jnp.exp(s[0] - top) for s in stats]
    total = functools.reduce(jnp.add, [r * s[1] for r, s in zip(ratios, stats)])
    return top, ratios, total


def merge_kernel(heads, up_ref, up_in_ref, down_ref, down_in_ref, up_out, down_out):
    for own, came, out, up in (
        (up_ref, up_in_ref, up_out, True),
        (down_ref, down_in_ref, down_out, False),
    ):
        width = came.shape[1]
        if width == own.shape[1]:
            lanes = slice(None)
        else:
            lanes = slice(0, width) if up else slice(width, 2 * width)
            rest = slice(width, 2 * width) if up else slice(0, width)
            out[:, rest] = own[:, rest]
        top, ratios, total = merged(heads, ((own, lanes), (came, slice(None))))
        for h in range(heads):
            cols = pl.ds(h * HD, HD)
            one = own[cols, lanes].astype(jnp.float32) * ratios[0][h : h + 1]
            two = came[cols, :].astype(jnp.float32) * ratios[1][h : h + 1]
            out[cols, lanes] = (one + two).astype(jnp.bfloat16)
        write_stats(out, lanes, heads, top, total)


def merge(up, up_in, down, down_in):
    heads = (up.shape[0] - STATS) // HD
    whole = jax.ShapeDtypeStruct(up.shape, jnp.bfloat16)
    return pl.pallas_call(
        functools.partial(merge_kernel, heads),
        out_shape=(whole, whole),
        compiler_params=PARAMS,
        cost_estimate=pl.CostEstimate(
            flops=1000000, bytes_accessed=2 * 1024 * 1024, transcendentals=1000
        ),
    )(up, up_in, down, down_in)


def last_kernel(heads, own_ref, up_ref, down_ref, out_ref):
    refs = (own_ref, up_ref, down_ref)
    _, ratios, total = merged(heads, [(ref, slice(None)) for ref in refs])
    valid = iota(total.shape, 0) < heads
    scales = [r / jnp.where(valid, total, 1.0) for r in ratios]
    for h in range(heads):
        cols = pl.ds(h * HD, HD)
        whole = jnp.zeros((HD, TOKENS), jnp.float32)
        for ref, scale in zip(refs, scales):
            whole = whole + ref[cols].astype(jnp.float32) * scale[h : h + 1]
        out_ref[:, cols] = jnp.transpose(whole).astype(out_ref.dtype)


def last(own, up, down):
    columns = own.shape[0] - STATS
    return pl.pallas_call(
        functools.partial(last_kernel, columns // HD),
        out_shape=jax.ShapeDtypeStruct((TOKENS, columns), jnp.bfloat16),
        compiler_params=PARAMS,
    )(own, up, down)


def body(queries, key_tokens, value_tokens, pair_keys, pair_count):
    tok_rows, columns = queries.shape
    assert lax.axis_size("ctx") == NX * NZ * NC
    assert tok_rows == TOKENS and pair_keys.shape == (BLOCKS, SLOTS)
    me = lax.axis_index("ctx")
    position = jnp.stack((me // (NZ * NC), (me // NC) % NZ, me % NC)).astype(jnp.int32)
    barrier = lax.optimization_barrier

    usable = jnp.arange(SLOTS, dtype=jnp.int32)[None, :] < pair_count[:, None]
    asked = jnp.concatenate(
        (jnp.where(usable, pair_keys // BLOCKS, -1), pair_keys % BLOCKS), axis=0
    ).astype(jnp.bfloat16)
    asked = jnp.pad(asked, ((0, 0), (0, columns - SLOTS)))
    pay = jnp.concatenate((queries[:HALF], asked, queries[HALF:]), axis=0)

    split = TOKENS + MEANS
    def means(tokens):
        grouped = tokens.reshape(BLOCKS, BLOCK, columns).astype(jnp.float32)
        return jnp.mean(grouped, axis=1).astype(jnp.bfloat16)

    own = jnp.concatenate(
        (key_tokens, means(key_tokens), means(value_tokens), value_tokens), axis=0
    )
    up1, down1 = move(pay, dz=1), move(pay, dz=-1)
    left, right = move(own, dx=1), move(own, dx=-1)
    own_twin = move(own, dc=1)
    up2, down2 = move(up1, dz=1), move(down1, dz=-1)
    far_k, far_v = move(left[:split], dx=1), move(right[split:], dx=-1)
    left_twin, right_twin = move(left, dc=1), move(right, dc=1)
    up3, down3 = move(up2, dz=1), move(down2, dz=-1)
    far_k_twin, far_v_twin = move(far_k, dc=1), move(far_v, dc=1)
    far_up = move(up3[: HALF + REQUEST], dz=1)
    far_down = move(down3[HALF:], dz=-1)
    far_up, far_down = barrier((far_up, far_down))
    key_refs = (own, own_twin, right, right_twin, far_k, far_k_twin, left, left_twin)
    value_refs = (own, own_twin, right, right_twin, far_v, far_v_twin, left, left_twin)
    plane = (*gather_means(key_refs), key_refs, value_refs)
    payloads = (pay, up1, down1, up2, down2, up3, down3)
    requests = [p[HALF : HALF + REQUEST, :HD] for p in payloads]
    tables = len(payloads)
    near = make_lists(
        position,
        jnp.concatenate(requests, axis=0),
        0,
        tables,
        tuple((table, 0, BLOCKS) for table in range(tables)),
    )
    both, mid = (0, HALF + REQUEST), BLOCKS // 2
    far = make_lists(position, far_up, HALF, 1, ((0, 0, mid), (0, mid, BLOCKS)))

    up_in, down_in = part(
        plane, *far, (far_up, far_down), (((0,), 0, mid, 0, 0), ((REQUEST,), mid, mid, 1, 0))
    )
    up_in, down_in = move(up_in, dz=-1), move(down_in, dz=1)
    for hop, up, down in ((3, up3, down3), (2, up2, down2), (1, up1, down1)):
        first = 2 * hop - 1
        groups = tuple((both, 0, BLOCKS, first + i, first + i) for i in range(2))
        up_part, down_part = part(plane, *near, (up, down), groups)
        up_sum, down_sum = merge(up_part, up_in, down_part, down_in)
        up_in, down_in = move(up_sum, dz=-1), move(down_sum, dz=1)
    (own_part,) = part(plane, *near, (pay,), ((both, 0, BLOCKS, 0, 0),))
    return last(own_part, up_in, down_in)


def solution(mesh):
    placed = (P("ctx", "head"), P("ctx", "head"), P("ctx", "head"), P("ctx", None), P("ctx"))
    return jax.shard_map(
        body, mesh=mesh, in_specs=placed, out_specs=P("ctx", "head"), check_vma=False
    )
```

```python
import functools
import math

import jax
import jax.numpy as jnp
from jax import lax
from jax.experimental import pallas as pl
from jax.experimental.pallas import tpu as pltpu
from jax.sharding import PartitionSpec as P

HD = 128
BLOCK = 32
NX, NZ, NC = 4, 8, 2
BLOCKS = 8
SLOTS = 4
TOKENS = BLOCKS * BLOCK
HALF = TOKENS // 2
REQUEST = 16
STATS = 32
MEANS = 16
PLANE = NX * NC
MOST = 2 * PLANE
FIRST = 2
CHUNK = 4
NEGATIVE = -1e30
ROWS_ROWS = (((1,), (1,)), ((), ()))
COLS_COLS = (((0,), (0,)), ((), ()))
PARAMS = pltpu.CompilerParams(vmem_limit_bytes=10 * 1024 * 1024)


def move(array, dx=0, dz=0, dc=0):
    pairs = []
    for x in range(NX):
        for z in range(NZ):
            for c in range(NC):
                to = (((x + dx) % NX) * NZ + (z + dz) % NZ) * NC + (c ^ dc)
                pairs.append(((x * NZ + z) * NC + c, to))
    return lax.ppermute(array, "ctx", pairs)


def iota(shape, axis):
    return lax.broadcasted_iota(jnp.int32, shape, axis)


ENTRY = 32
MEAN_KEYS = PLANE * BLOCKS


def list_kernel(first, spec, pos_ref, asked_ref, bias_ref, list_ref, ids_vmem, ids_ref, sem):
    mx, mz, mc = pos_ref[0], pos_ref[1], pos_ref[2]
    tables = ids_vmem.shape[0]
    row = iota((BLOCKS, HD), 0)
    for table in range(tables):
        rows = pl.ds(first + table * REQUEST, REQUEST)
        request = asked_ref[rows, :HD].astype(jnp.float32)
        owner, within = request[:BLOCKS].astype(jnp.int32), request[BLOCKS:].astype(jnp.int32)
        here = (owner >= 0) & (((owner >> 1) & (NZ - 1)) == mz)
        rel = (((owner >> 4) - mx) & (NX - 1)) * NC + ((owner & 1) ^ mc)
        ids_vmem[table] = jnp.where(here, (row * PLANE + rel) * BLOCKS + within, -1)
    ids_copy = pltpu.make_async_copy(ids_vmem, ids_ref, sem)
    ids_copy.start()
    ids_copy.wait()

    for g, (table, low, high) in enumerate(spec):
        for n in range(FIRST + MOST):
            list_ref[g, ENTRY + n] = -1
        used = jnp.int32(0)
        for b in range(low, high):
            for p in range(SLOTS):
                code = ids_ref[table, b, p]
                list_ref[g, ENTRY + used] = code
                used = used + (code >= 0).astype(jnp.int32)
        list_ref[g, 0] = used

    shape = (MEAN_KEYS, TOKENS)
    key_ids, token_blocks = iota(shape, 0), iota(shape, 1) // BLOCK
    for table in range(tables):
        bias = jnp.full(shape, math.log(BLOCK), jnp.float32)
        for g in range(len(spec)):
            if spec[g][0] != table:
                continue

            def exclude(n, bias, g=g):
                code = list_ref[g, ENTRY + n]
                hit = (key_ids == (code & (MEAN_KEYS - 1))) & (token_blocks == code >> 6)
                return jnp.where(hit, NEGATIVE, bias)

            bias = lax.fori_loop(0, list_ref[g, 0], exclude, bias)
        bias_ref[table] = bias


def make_lists(position, asked, first, tables, spec):
    vmem = pl.BlockSpec(memory_space=pltpu.VMEM)
    smem = pl.BlockSpec(memory_space=pltpu.SMEM)
    return pl.pallas_call(
        functools.partial(list_kernel, first, spec),
        in_specs=[smem, vmem],
        out_specs=[vmem, smem],
        out_shape=[
            jax.ShapeDtypeStruct((tables, MEAN_KEYS, TOKENS), jnp.float32),
            jax.ShapeDtypeStruct((len(spec), HD), jnp.int32),
        ],
        scratch_shapes=[
            pltpu.VMEM((tables, BLOCKS, HD), jnp.int32),
            pltpu.SMEM((tables, BLOCKS, HD), jnp.int32),
            pltpu.SemaphoreType.DMA,
        ],
        compiler_params=PARAMS,
        cost_estimate=pl.CostEstimate(flops=1000000, bytes_accessed=1024 * 1024, transcendentals=0),
    )(position, asked)


def means_kernel(*refs):
    sources, (mean_k_ref, mean_v_ref) = refs[:PLANE], refs[PLANE:]
    tiles = [source[TOKENS : TOKENS + MEANS].astype(jnp.float32) for source in sources]
    mean_k_ref[...] = jnp.concatenate([t[:BLOCKS] for t in tiles], axis=0).astype(jnp.bfloat16)
    mean_v_ref[...] = jnp.concatenate([t[BLOCKS:] for t in tiles], axis=0).astype(jnp.bfloat16)


def gather_means(sources):
    shape = jax.ShapeDtypeStruct((MEAN_KEYS, sources[0].shape[1]), jnp.bfloat16)
    return pl.pallas_call(
        means_kernel,
        out_shape=(shape, shape),
        compiler_params=PARAMS,
        cost_estimate=pl.CostEstimate(flops=1000000, bytes_accessed=1024 * 1024, transcendentals=0),
    )(*sources)


def own_kernel(key_ref, value_ref, out_ref, sem):
    split = TOKENS + MEANS
    starts = (0, split)
    copies = []
    for n, ref in enumerate((key_ref, value_ref)):
        target = out_ref.at[pl.ds(starts[n], TOKENS)]
        copies.append(pltpu.make_async_copy(ref, target, sem.at[n]))
        copies[n].start()
    means = []
    for first, copy in zip(starts, copies):
        copy.wait()
        for b in range(BLOCKS):
            rows = pl.ds(first + b * BLOCK, BLOCK)
            block = out_ref[rows].astype(jnp.float32)
            means.append(jnp.sum(block, axis=0, keepdims=True) * (1.0 / BLOCK))
    out_ref[TOKENS:split] = jnp.concatenate(means, axis=0).astype(jnp.bfloat16)


def make_own(keys, values):
    rows = 2 * TOKENS + MEANS
    return pl.pallas_call(
        own_kernel,
        in_specs=[pl.BlockSpec(memory_space=pl.ANY)] * 2,
        out_shape=jax.ShapeDtypeStruct((rows, keys.shape[1]), jnp.bfloat16),
        scratch_shapes=[pltpu.SemaphoreType.DMA((2,))],
        compiler_params=PARAMS,
    )(keys, values)


def part_kernel(heads, groups, list_ref, mean_k_ref, mean_v_ref, bias_ref, *rest):
    count = len(groups)
    key_refs, rest = rest[:PLANE], rest[PLANE:]
    value_refs, rest = rest[:PLANE], rest[PLANE:]
    q_refs, rest = rest[:count], rest[count:]
    out_refs = []
    for group in groups:
        halves = group[2] * BLOCK // HALF
        out_refs.append(rest[:halves])
        rest = rest[halves:]
    accs, rest = rest[:count], rest[count:]
    tops, rest = rest[:count], rest[count:]
    sums, bufs = rest[:count], rest[count:]
    inv_root = 1.0 / math.sqrt(HD)
    chunks = []
    for g in range(count):
        which = groups[g][3]
        used = list_ref[which, 0]
        chunks.append((jnp.maximum(used - FIRST, 0) + CHUNK - 1) // CHUNK)

        def fetch(n, carry, g=g, which=which):
            key = list_ref[which, ENTRY + n] & (MEAN_KEYS - 1)
            first = pl.multiple_of((key % BLOCKS) * BLOCK, BLOCK)
            for i in range(PLANE):

                @pl.when(key // BLOCKS == i)
                def _(i=i):
                    skip = value_refs[i].shape[0] - TOKENS
                    rows = pl.ds(pl.multiple_of(first + skip, 16), BLOCK)
                    bufs[g][n, :BLOCK] = key_refs[i][pl.ds(first, BLOCK)]
                    bufs[g][n, BLOCK:] = value_refs[i][rows]

            return carry

        lax.fori_loop(0, FIRST + CHUNK * chunks[g], fetch, 0)

    def slots_of(g, first, number):
        _, low, blocks, which, _ = groups[g]
        token_blocks = iota((1, blocks * BLOCK), 1) // BLOCK + low
        places, rows = [], []
        for j in range(number):
            code = list_ref[which, ENTRY + first + j]
            places.append((g, first + j))
            rows.append(jnp.where(token_blocks == code >> 6, 0.0, NEGATIVE))
        return places, rows

    def keys_of(places, cols):
        return [bufs[g][n, :BLOCK, cols] for g, n in places]

    def values_of(places, cols):
        return [bufs[g][n, BLOCK:, cols] for g, n in places]

    def logits_of(g, keys, cols, biases):
        pieces = [q_refs[g][row : row + HALF, cols] for row in groups[g][0]]
        queries = pieces[0] if len(pieces) == 1 else jnp.concatenate(pieces, axis=0)
        logits = lax.dot_general(
            jnp.concatenate(keys, axis=0), queries, ROWS_ROWS, preferred_element_type=jnp.float32
        )
        logits = logits * inv_root
        pieces, row = [], 0
        for key, bias in zip(keys, biases):
            pieces.append(logits[row : row + key.shape[0]] + bias)
            row += key.shape[0]
        return jnp.concatenate(pieces, axis=0)

    def summed(values, weights):
        return lax.dot_general(
            jnp.concatenate(values, axis=0),
            weights,
            COLS_COLS,
            preferred_element_type=jnp.float32,
        )

    all_cols = [pl.ds(h * HD, HD) for h in range(heads)]
    for g in range(count):
        _, low, blocks, _, table = groups[g]
        places, rows = slots_of(g, 0, FIRST)
        bias = bias_ref[table, :, low * BLOCK : (low + blocks) * BLOCK]
        tiles = [
            logits_of(g, [mean_k_ref[:, cols]] + keys_of(places, cols), cols, [bias] + rows)
            for cols in all_cols
        ]
        for h, cols in enumerate(all_cols):
            top = jnp.max(tiles[h], axis=0, keepdims=True)
            weights = jnp.exp(tiles[h] - top)
            tops[g][h : h + 1] = top
            sums[g][h : h + 1] = jnp.sum(weights, axis=0, keepdims=True)
            tiles[h] = weights.astype(jnp.bfloat16)
        for h, cols in enumerate(all_cols):
            accs[g][cols] = summed([mean_v_ref[:, cols]] + values_of(places, cols), tiles[h])

    for g in range(count):

        def chunk(ci, carry, g=g):
            places, rows = slots_of(g, FIRST + ci * CHUNK, CHUNK)
            tiles = [logits_of(g, keys_of(places, cols), cols, rows) for cols in all_cols]
            ratios = []
            for h in range(heads):
                before = tops[g][h : h + 1]
                top = jnp.maximum(before, jnp.max(tiles[h], axis=0, keepdims=True))
                weights = jnp.exp(tiles[h] - top)
                ratio = jnp.exp(before - top)
                tops[g][h : h + 1] = top
                sums[g][h : h + 1] = sums[g][h : h + 1] * ratio + jnp.sum(
                    weights, axis=0, keepdims=True
                )
                tiles[h] = weights.astype(jnp.bfloat16)
                ratios.append(ratio)
            for h, cols in enumerate(all_cols):
                accs[g][cols] = accs[g][cols] * ratios[h] + summed(
                    values_of(places, cols), tiles[h]
                )
            return carry

        lax.fori_loop(0, chunks[g], chunk, 0)

    for g in range(count):
        top = tops[g][...]
        sent = top.astype(jnp.bfloat16).astype(jnp.float32)
        factor = jnp.exp(top - sent)
        total = sums[g][...] * factor
        for half, out_ref in enumerate(out_refs[g]):
            lanes = slice(half * HALF, (half + 1) * HALF)
            for h, cols in enumerate(all_cols):
                out_ref[cols] = (accs[g][cols, lanes] * factor[h : h + 1, lanes]).astype(jnp.bfloat16)
            write_stats(out_ref, heads, sent[:, lanes], total[:, lanes])


def write_stats(out_ref, heads, top, total):
    high = total.astype(jnp.bfloat16).astype(jnp.float32)
    rows = (top, high, total - high, jnp.zeros_like(top))
    valid = iota(top.shape, 0) < heads
    rows = [jnp.where(valid, r, 0.0) for r in rows]
    out_ref[heads * HD :] = jnp.concatenate(rows, axis=0).astype(jnp.bfloat16)


def part(plane, bias, lists, queries, groups):
    columns = queries[0].shape[1]
    heads = columns // HD
    vmem = pl.BlockSpec(memory_space=pltpu.VMEM)
    smem = pl.BlockSpec(memory_space=pltpu.SMEM)
    widths = [group[2] * BLOCK for group in groups]
    scratch = [pltpu.VMEM((columns, w), jnp.float32) for w in widths]
    scratch += [pltpu.VMEM((8, w), jnp.float32) for w in widths] * 2
    scratch += [pltpu.VMEM((FIRST + MOST, 2 * BLOCK, columns), jnp.bfloat16) for _ in widths]
    mean_k, mean_v, key_refs, value_refs = plane
    operands = (mean_k, mean_v, bias, *key_refs, *value_refs, *queries)
    return pl.pallas_call(
        functools.partial(part_kernel, heads, groups),
        in_specs=[smem] + [vmem] * len(operands),
        out_specs=[vmem] * (sum(widths) // HALF),
        out_shape=[jax.ShapeDtypeStruct((columns + STATS, HALF), jnp.bfloat16)]
        * (sum(widths) // HALF),
        scratch_shapes=scratch,
        compiler_params=PARAMS,
        cost_estimate=pl.CostEstimate(
            flops=4 * 512 * 1024 * columns, bytes_accessed=4 * 1024 * 1024, transcendentals=500000
        ),
    )(lists, *operands)


def merged(heads, refs):
    stats = [ref[heads * HD :].astype(jnp.float32) for ref in refs]
    top = functools.reduce(jnp.maximum, [s[:8] for s in stats])
    ratios = [jnp.exp(s[:8] - top) for s in stats]
    totals = [r * (s[8:16] + s[16:24]) for r, s in zip(ratios, stats)]
    return top, ratios, functools.reduce(jnp.add, totals)


def merge_kernel(heads, *refs):
    count = len(refs) // 3
    for own, came, out in zip(refs[:count], refs[count : 2 * count], refs[2 * count :]):
        top, ratios, total = merged(heads, (own, came))
        for h in range(heads):
            cols = pl.ds(h * HD, HD)
            one = own[cols].astype(jnp.float32) * ratios[0][h : h + 1]
            two = came[cols].astype(jnp.float32) * ratios[1][h : h + 1]
            out[cols] = (one + two).astype(jnp.bfloat16)
        write_stats(out, heads, top, total)


def merge(owns, cames):
    heads = (owns[0].shape[0] - STATS) // HD
    return pl.pallas_call(
        functools.partial(merge_kernel, heads),
        out_shape=[jax.ShapeDtypeStruct(own.shape, jnp.bfloat16) for own in owns],
        compiler_params=PARAMS,
        cost_estimate=pl.CostEstimate(
            flops=1000000, bytes_accessed=1024 * 1024, transcendentals=1000
        ),
    )(*owns, *cames)


def last_kernel(heads, *refs):
    out_ref = refs[-1]
    for half in range(2):
        parts = refs[half : len(refs) - 1 : 2]
        _, ratios, total = merged(heads, parts)
        valid = iota(total.shape, 0) < heads
        scales = [r / jnp.where(valid, total, 1.0) for r in ratios]
        rows = pl.ds(half * HALF, HALF)
        for h in range(heads):
            cols = pl.ds(h * HD, HD)
            whole = jnp.zeros((HD, HALF), jnp.float32)
            for ref, scale in zip(parts, scales):
                whole = whole + ref[cols].astype(jnp.float32) * scale[h : h + 1]
            out_ref[rows, cols] = jnp.transpose(whole).astype(out_ref.dtype)


def last(parts):
    columns = parts[0].shape[0] - STATS
    return pl.pallas_call(
        functools.partial(last_kernel, columns // HD),
        out_shape=jax.ShapeDtypeStruct((TOKENS, columns), jnp.bfloat16),
        compiler_params=PARAMS,
    )(*parts)


def body(queries, key_tokens, value_tokens, pair_keys, pair_count):
    tok_rows, columns = queries.shape
    assert lax.axis_size("ctx") == NX * NZ * NC
    assert tok_rows == TOKENS and pair_keys.shape == (BLOCKS, SLOTS)
    me = lax.axis_index("ctx")
    position = jnp.stack((me // (NZ * NC), (me // NC) % NZ, me % NC)).astype(jnp.int32)
    barrier = lax.optimization_barrier

    usable = jnp.arange(SLOTS, dtype=jnp.int32)[None, :] < pair_count[:, None]
    asked = jnp.concatenate(
        (jnp.where(usable, pair_keys // BLOCKS, -1), pair_keys % BLOCKS), axis=0
    ).astype(jnp.bfloat16)
    asked = jnp.pad(asked, ((0, 0), (0, columns - SLOTS)))
    pay = jnp.concatenate((queries[:HALF], asked, queries[HALF:]), axis=0)

    split = TOKENS + MEANS
    def means(tokens):
        grouped = tokens.reshape(BLOCKS, BLOCK, columns).astype(jnp.float32)
        return jnp.mean(grouped, axis=1).astype(jnp.bfloat16)

    own = jnp.concatenate(
        (key_tokens, means(key_tokens), means(value_tokens), value_tokens), axis=0
    )
    up1, down1 = move(pay, dz=1), move(pay, dz=-1)
    left, right = move(own, dx=1), move(own, dx=-1)
    own_twin = move(own, dc=1)
    up2, down2 = move(up1, dz=1), move(down1, dz=-1)
    far_k, far_v = move(left[:split], dx=1), move(right[split:], dx=-1)
    left_twin, right_twin = move(left, dc=1), move(right, dc=1)
    up3, down3 = move(up2, dz=1), move(down2, dz=-1)
    far_up = move(up3[: HALF + REQUEST], dz=1)
    far_down = move(down3[HALF:], dz=-1)
    payloads = (pay, up1, down1, up2, down2, up3, down3)
    requests = [p[HALF : HALF + REQUEST, :HD] for p in payloads]
    tables = len(payloads)
    near = make_lists(
        position,
        jnp.concatenate(requests, axis=0),
        0,
        tables,
        tuple((table, 0, BLOCKS) for table in range(tables)),
    )
    far_k, far_v, *near = barrier((far_k, far_v, *near))
    far_k_twin, far_v_twin = move(far_k, dc=1), move(far_v, dc=1)
    key_refs = (own, own_twin, right, right_twin, far_k, far_k_twin, left, left_twin)
    value_refs = (own, own_twin, right, right_twin, far_v, far_v_twin, left, left_twin)
    plane = (*gather_means(key_refs), key_refs, value_refs)
    far_up, far_down = barrier((far_up, far_down))
    both, mid = (0, HALF + REQUEST), BLOCKS // 2
    far = make_lists(position, far_up, HALF, 1, ((0, 0, mid), (0, mid, BLOCKS)))

    up_a, down_b = part(
        plane, *far, (far_up, far_down), (((0,), 0, mid, 0, 0), ((REQUEST,), mid, mid, 1, 0))
    )
    up_a, down_b = move(up_a, dz=-1), move(down_b, dz=1)
    up_b = down_a = None
    for hop, up, down in ((3, up3, down3), (2, up2, down2), (1, up1, down1)):
        first = 2 * hop - 1
        groups = tuple((both, 0, BLOCKS, first + i, first + i) for i in range(2))
        own_up_a, own_up_b, own_down_a, own_down_b = part(plane, *near, (up, down), groups)
        if up_b is None:
            up_b, down_a = own_up_b, own_down_a
        else:
            up_b, down_a = merge((own_up_b, own_down_a), (up_b, down_a))
        up_b, down_a = move(up_b, dz=-1), move(down_a, dz=1)
        up_a, down_b = merge((own_up_a, own_down_b), (up_a, down_b))
        up_a, down_b = move(up_a, dz=-1), move(down_b, dz=1)
    own_a, own_b = part(plane, *near, (pay,), ((both, 0, BLOCKS, 0, 0),))
    return last((own_a, own_b, up_a, up_b, down_a, down_b))


def solution(mesh):
    placed = (P("ctx", "head"), P("ctx", "head"), P("ctx", "head"), P("ctx", None), P("ctx"))
    return jax.shard_map(
        body, mesh=mesh, in_specs=placed, out_specs=P("ctx", "head"), check_vma=False
    )
```

```python
import functools
import math

import jax
import jax.numpy as jnp
from jax import lax
from jax.experimental import pallas as pl
from jax.experimental.pallas import tpu as pltpu
from jax.sharding import PartitionSpec as P

HD = 128
BLOCK = 32
NX, NZ, NC = 4, 8, 2
BLOCKS = 8
SLOTS = 4
TOKENS = BLOCKS * BLOCK
HALF = TOKENS // 2
REQUEST = 16
STATS = 32
MEANS = 16
PLANE = NX * NC
MOST = 2 * PLANE
FIRST = 4
CHUNK = 4
NEGATIVE = -1e30
ROWS_ROWS = (((1,), (1,)), ((), ()))
COLS_COLS = (((0,), (0,)), ((), ()))
PARAMS = pltpu.CompilerParams(vmem_limit_bytes=10 * 1024 * 1024)


def move(array, dx=0, dz=0, dc=0):
    pairs = []
    for x in range(NX):
        for z in range(NZ):
            for c in range(NC):
                to = (((x + dx) % NX) * NZ + (z + dz) % NZ) * NC + (c ^ dc)
                pairs.append(((x * NZ + z) * NC + c, to))
    return lax.ppermute(array, "ctx", pairs)


def iota(shape, axis):
    return lax.broadcasted_iota(jnp.int32, shape, axis)


ENTRY = 32
MEAN_KEYS = PLANE * BLOCKS


def list_kernel(first, spec, pos_ref, asked_ref, bias_ref, list_ref, ids_vmem, ids_ref, sem):
    mx, mz, mc = pos_ref[0], pos_ref[1], pos_ref[2]
    tables = ids_vmem.shape[0]
    row = iota((BLOCKS, HD), 0)
    for table in range(tables):
        rows = pl.ds(first + table * REQUEST, REQUEST)
        request = asked_ref[rows, :HD].astype(jnp.float32)
        owner, within = request[:BLOCKS].astype(jnp.int32), request[BLOCKS:].astype(jnp.int32)
        here = (owner >= 0) & (((owner >> 1) & (NZ - 1)) == mz)
        rel = (((owner >> 4) - mx) & (NX - 1)) * NC + ((owner & 1) ^ mc)
        ids_vmem[table] = jnp.where(here, (row * PLANE + rel) * BLOCKS + within, -1)
    ids_copy = pltpu.make_async_copy(ids_vmem, ids_ref, sem)
    ids_copy.start()
    ids_copy.wait()

    for g, (table, low, high) in enumerate(spec):
        for n in range(FIRST + MOST):
            list_ref[g, ENTRY + n] = -1
        used = jnp.int32(0)
        for b in range(low, high):
            for p in range(SLOTS):
                code = ids_ref[table, b, p]
                list_ref[g, ENTRY + used] = code
                used = used + (code >= 0).astype(jnp.int32)
        list_ref[g, 0] = used

    shape = (MEAN_KEYS, TOKENS)
    key_ids, token_blocks = iota(shape, 0), iota(shape, 1) // BLOCK
    for table in range(tables):
        bias = jnp.full(shape, math.log(BLOCK), jnp.float32)
        for g in range(len(spec)):
            if spec[g][0] != table:
                continue

            def exclude(n, bias, g=g):
                code = list_ref[g, ENTRY + n]
                hit = (key_ids == (code & (MEAN_KEYS - 1))) & (token_blocks == code >> 6)
                return jnp.where(hit, NEGATIVE, bias)

            bias = lax.fori_loop(0, list_ref[g, 0], exclude, bias)
        bias_ref[table] = bias


def make_lists(position, asked, first, tables, spec):
    vmem = pl.BlockSpec(memory_space=pltpu.VMEM)
    smem = pl.BlockSpec(memory_space=pltpu.SMEM)
    return pl.pallas_call(
        functools.partial(list_kernel, first, spec),
        in_specs=[smem, vmem],
        out_specs=[vmem, smem],
        out_shape=[
            jax.ShapeDtypeStruct((tables, MEAN_KEYS, TOKENS), jnp.float32),
            jax.ShapeDtypeStruct((len(spec), HD), jnp.int32),
        ],
        scratch_shapes=[
            pltpu.VMEM((tables, BLOCKS, HD), jnp.int32),
            pltpu.SMEM((tables, BLOCKS, HD), jnp.int32),
            pltpu.SemaphoreType.DMA,
        ],
        compiler_params=PARAMS,
        cost_estimate=pl.CostEstimate(flops=1000000, bytes_accessed=1024 * 1024, transcendentals=0),
    )(position, asked)


def means_kernel(*refs):
    sources, (mean_k_ref, mean_v_ref) = refs[:PLANE], refs[PLANE:]
    tiles = [source[TOKENS : TOKENS + MEANS].astype(jnp.float32) for source in sources]
    mean_k_ref[...] = jnp.concatenate([t[:BLOCKS] for t in tiles], axis=0).astype(jnp.bfloat16)
    mean_v_ref[...] = jnp.concatenate([t[BLOCKS:] for t in tiles], axis=0).astype(jnp.bfloat16)


def cut_kernel(up_ref, down_ref, up_out, down_out):
    up_out[...] = up_ref[: HALF + REQUEST]
    down_out[...] = down_ref[HALF:]


def cut(up, down):
    shape = jax.ShapeDtypeStruct((HALF + REQUEST, up.shape[1]), up.dtype)
    return pl.pallas_call(cut_kernel, out_shape=(shape, shape), compiler_params=PARAMS)(up, down)


def gather_means(sources):
    shape = jax.ShapeDtypeStruct((MEAN_KEYS, sources[0].shape[1]), jnp.bfloat16)
    return pl.pallas_call(
        means_kernel,
        out_shape=(shape, shape),
        compiler_params=PARAMS,
        cost_estimate=pl.CostEstimate(flops=1000000, bytes_accessed=1024 * 1024, transcendentals=0),
    )(*sources)


def own_kernel(key_ref, value_ref, out_ref, sem):
    split = TOKENS + MEANS
    starts = (0, split)
    copies = []
    for n, ref in enumerate((key_ref, value_ref)):
        target = out_ref.at[pl.ds(starts[n], TOKENS)]
        copies.append(pltpu.make_async_copy(ref, target, sem.at[n]))
        copies[n].start()
    means = []
    for first, copy in zip(starts, copies):
        copy.wait()
        for b in range(BLOCKS):
            rows = pl.ds(first + b * BLOCK, BLOCK)
            block = out_ref[rows].astype(jnp.float32)
            means.append(jnp.sum(block, axis=0, keepdims=True) * (1.0 / BLOCK))
    out_ref[TOKENS:split] = jnp.concatenate(means, axis=0).astype(jnp.bfloat16)


def make_own(keys, values):
    rows = 2 * TOKENS + MEANS
    return pl.pallas_call(
        own_kernel,
        in_specs=[pl.BlockSpec(memory_space=pl.ANY)] * 2,
        out_shape=jax.ShapeDtypeStruct((rows, keys.shape[1]), jnp.bfloat16),
        scratch_shapes=[pltpu.SemaphoreType.DMA((2,))],
        compiler_params=PARAMS,
    )(keys, values)


def part_kernel(heads, groups, list_ref, mean_k_ref, mean_v_ref, bias_ref, *rest):
    count = len(groups)
    key_refs, rest = rest[:PLANE], rest[PLANE:]
    value_refs, rest = rest[:PLANE], rest[PLANE:]
    q_refs, rest = rest[:count], rest[count:]
    out_refs = []
    for group in groups:
        halves = group[2] * BLOCK // HALF
        out_refs.append(rest[:halves])
        rest = rest[halves:]
    accs, rest = rest[:count], rest[count:]
    tops, rest = rest[:count], rest[count:]
    sums, bufs = rest[:count], rest[count:]
    inv_root = 1.0 / math.sqrt(HD)
    chunks = []
    for g in range(count):
        which = groups[g][3]
        used = list_ref[which, 0]
        chunks.append((jnp.maximum(used - FIRST, 0) + CHUNK - 1) // CHUNK)

        def fetch(n, carry, g=g, which=which):
            key = list_ref[which, ENTRY + n] & (MEAN_KEYS - 1)
            first = pl.multiple_of((key % BLOCKS) * BLOCK, BLOCK)
            for i in range(PLANE):

                @pl.when(key // BLOCKS == i)
                def _(i=i):
                    skip = value_refs[i].shape[0] - TOKENS
                    rows = pl.ds(pl.multiple_of(first + skip, 16), BLOCK)
                    bufs[g][n, :BLOCK] = key_refs[i][pl.ds(first, BLOCK)]
                    bufs[g][n, BLOCK:] = value_refs[i][rows]

            return carry

        lax.fori_loop(0, FIRST + CHUNK * chunks[g], fetch, 0)

    def slots_of(g, first, number):
        _, low, blocks, which, _ = groups[g]
        token_blocks = iota((1, blocks * BLOCK), 1) // BLOCK + low
        places, rows = [], []
        for j in range(number):
            code = list_ref[which, ENTRY + first + j]
            places.append((g, first + j))
            rows.append(jnp.where(token_blocks == code >> 6, 0.0, NEGATIVE))
        return places, rows

    def keys_of(places, cols):
        return [bufs[g][n, :BLOCK, cols] for g, n in places]

    def values_of(places, cols):
        return [bufs[g][n, BLOCK:, cols] for g, n in places]

    def logits_of(g, keys, cols, biases):
        pieces = [q_refs[g][row : row + HALF, cols] for row in groups[g][0]]
        queries = pieces[0] if len(pieces) == 1 else jnp.concatenate(pieces, axis=0)
        logits = lax.dot_general(
            jnp.concatenate(keys, axis=0), queries, ROWS_ROWS, preferred_element_type=jnp.float32
        )
        logits = logits * inv_root
        pieces, row = [], 0
        for key, bias in zip(keys, biases):
            pieces.append(logits[row : row + key.shape[0]] + bias)
            row += key.shape[0]
        return jnp.concatenate(pieces, axis=0)

    def summed(values, weights):
        return lax.dot_general(
            jnp.concatenate(values, axis=0),
            weights,
            COLS_COLS,
            preferred_element_type=jnp.float32,
        )

    all_cols = [pl.ds(h * HD, HD) for h in range(heads)]
    for g in range(count):
        _, low, blocks, _, table = groups[g]
        places, rows = slots_of(g, 0, FIRST)
        bias = bias_ref[table, :, low * BLOCK : (low + blocks) * BLOCK]
        tiles = [
            logits_of(g, [mean_k_ref[:, cols]] + keys_of(places, cols), cols, [bias] + rows)
            for cols in all_cols
        ]
        for h, cols in enumerate(all_cols):
            top = jnp.max(tiles[h], axis=0, keepdims=True)
            weights = jnp.exp(tiles[h] - top)
            tops[g][h : h + 1] = top
            sums[g][h : h + 1] = jnp.sum(weights, axis=0, keepdims=True)
            tiles[h] = weights.astype(jnp.bfloat16)
        for h, cols in enumerate(all_cols):
            accs[g][cols] = summed([mean_v_ref[:, cols]] + values_of(places, cols), tiles[h])

    for g in range(count):

        def chunk(ci, carry, g=g):
            places, rows = slots_of(g, FIRST + ci * CHUNK, CHUNK)
            tiles = [logits_of(g, keys_of(places, cols), cols, rows) for cols in all_cols]
            ratios = []
            for h in range(heads):
                before = tops[g][h : h + 1]
                top = jnp.maximum(before, jnp.max(tiles[h], axis=0, keepdims=True))
                weights = jnp.exp(tiles[h] - top)
                ratio = jnp.exp(before - top)
                tops[g][h : h + 1] = top
                sums[g][h : h + 1] = sums[g][h : h + 1] * ratio + jnp.sum(
                    weights, axis=0, keepdims=True
                )
                tiles[h] = weights.astype(jnp.bfloat16)
                ratios.append(ratio)
            for h, cols in enumerate(all_cols):
                accs[g][cols] = accs[g][cols] * ratios[h] + summed(
                    values_of(places, cols), tiles[h]
                )
            return carry

        lax.fori_loop(0, chunks[g], chunk, 0)

    for g in range(count):
        top = tops[g][...]
        sent = top.astype(jnp.bfloat16).astype(jnp.float32)
        factor = jnp.exp(top - sent)
        total = sums[g][...] * factor
        for half, out_ref in enumerate(out_refs[g]):
            lanes = slice(half * HALF, (half + 1) * HALF)
            for h, cols in enumerate(all_cols):
                out_ref[cols] = (accs[g][cols, lanes] * factor[h : h + 1, lanes]).astype(jnp.bfloat16)
            write_stats(out_ref, heads, sent[:, lanes], total[:, lanes])


def write_stats(out_ref, heads, top, total):
    high = total.astype(jnp.bfloat16).astype(jnp.float32)
    rows = (top, high, total - high, jnp.zeros_like(top))
    valid = iota(top.shape, 0) < heads
    rows = [jnp.where(valid, r, 0.0) for r in rows]
    out_ref[heads * HD :] = jnp.concatenate(rows, axis=0).astype(jnp.bfloat16)


def part(plane, bias, lists, queries, groups):
    columns = queries[0].shape[1]
    heads = columns // HD
    vmem = pl.BlockSpec(memory_space=pltpu.VMEM)
    smem = pl.BlockSpec(memory_space=pltpu.SMEM)
    widths = [group[2] * BLOCK for group in groups]
    scratch = [pltpu.VMEM((columns, w), jnp.float32) for w in widths]
    scratch += [pltpu.VMEM((8, w), jnp.float32) for w in widths] * 2
    scratch += [pltpu.VMEM((FIRST + MOST, 2 * BLOCK, columns), jnp.bfloat16) for _ in widths]
    mean_k, mean_v, key_refs, value_refs = plane
    operands = (mean_k, mean_v, bias, *key_refs, *value_refs, *queries)
    return pl.pallas_call(
        functools.partial(part_kernel, heads, groups),
        in_specs=[smem] + [vmem] * len(operands),
        out_specs=[vmem] * (sum(widths) // HALF),
        out_shape=[jax.ShapeDtypeStruct((columns + STATS, HALF), jnp.bfloat16)]
        * (sum(widths) // HALF),
        scratch_shapes=scratch,
        compiler_params=PARAMS,
        cost_estimate=pl.CostEstimate(
            flops=4 * 512 * 1024 * columns, bytes_accessed=4 * 1024 * 1024, transcendentals=500000
        ),
    )(lists, *operands)


def merged(heads, refs):
    stats = [ref[heads * HD :].astype(jnp.float32) for ref in refs]
    top = functools.reduce(jnp.maximum, [s[:8] for s in stats])
    ratios = [jnp.exp(s[:8] - top) for s in stats]
    totals = [r * (s[8:16] + s[16:24]) for r, s in zip(ratios, stats)]
    return top, ratios, functools.reduce(jnp.add, totals)


def merge_kernel(heads, *refs):
    count = len(refs) // 3
    for own, came, out in zip(refs[:count], refs[count : 2 * count], refs[2 * count :]):
        top, ratios, total = merged(heads, (own, came))
        for h in range(heads):
            cols = pl.ds(h * HD, HD)
            one = own[cols].astype(jnp.float32) * ratios[0][h : h + 1]
            two = came[cols].astype(jnp.float32) * ratios[1][h : h + 1]
            out[cols] = (one + two).astype(jnp.bfloat16)
        write_stats(out, heads, top, total)


def merge(owns, cames):
    heads = (owns[0].shape[0] - STATS) // HD
    return pl.pallas_call(
        functools.partial(merge_kernel, heads),
        out_shape=[jax.ShapeDtypeStruct(own.shape, jnp.bfloat16) for own in owns],
        compiler_params=PARAMS,
        cost_estimate=pl.CostEstimate(
            flops=1000000, bytes_accessed=1024 * 1024, transcendentals=1000
        ),
    )(*owns, *cames)


def last_kernel(heads, *refs):
    out_ref = refs[-1]
    for half in range(2):
        parts = refs[half : len(refs) - 1 : 2]
        _, ratios, total = merged(heads, parts)
        valid = iota(total.shape, 0) < heads
        scales = [r / jnp.where(valid, total, 1.0) for r in ratios]
        rows = pl.ds(half * HALF, HALF)
        for h in range(heads):
            cols = pl.ds(h * HD, HD)
            whole = jnp.zeros((HD, HALF), jnp.float32)
            for ref, scale in zip(parts, scales):
                whole = whole + ref[cols].astype(jnp.float32) * scale[h : h + 1]
            out_ref[rows, cols] = jnp.transpose(whole).astype(out_ref.dtype)


def last(parts):
    columns = parts[0].shape[0] - STATS
    return pl.pallas_call(
        functools.partial(last_kernel, columns // HD),
        out_shape=jax.ShapeDtypeStruct((TOKENS, columns), jnp.bfloat16),
        compiler_params=PARAMS,
    )(*parts)


def body(queries, key_tokens, value_tokens, pair_keys, pair_count):
    tok_rows, columns = queries.shape
    assert lax.axis_size("ctx") == NX * NZ * NC
    assert tok_rows == TOKENS and pair_keys.shape == (BLOCKS, SLOTS)
    me = lax.axis_index("ctx")
    position = jnp.stack((me // (NZ * NC), (me // NC) % NZ, me % NC)).astype(jnp.int32)
    barrier = lax.optimization_barrier

    usable = jnp.arange(SLOTS, dtype=jnp.int32)[None, :] < pair_count[:, None]
    asked = jnp.concatenate(
        (jnp.where(usable, pair_keys // BLOCKS, -1), pair_keys % BLOCKS), axis=0
    ).astype(jnp.bfloat16)
    asked = jnp.pad(asked, ((0, 0), (0, columns - SLOTS)))
    pay = jnp.concatenate((queries[:HALF], asked, queries[HALF:]), axis=0)

    split = TOKENS + MEANS
    def means(tokens):
        grouped = tokens.reshape(BLOCKS, BLOCK, columns).astype(jnp.float32)
        return jnp.mean(grouped, axis=1).astype(jnp.bfloat16)

    own = jnp.concatenate(
        (key_tokens, means(key_tokens), means(value_tokens), value_tokens), axis=0
    )
    up1, down1 = move(pay, dz=1), move(pay, dz=-1)
    left, right = move(own, dx=1), move(own, dx=-1)
    own_twin = move(own, dc=1)
    up2, down2 = move(up1, dz=1), move(down1, dz=-1)
    far_k, far_v = move(left[:split], dx=1), move(right[split:], dx=-1)
    left_twin, right_twin = move(left, dc=1), move(right, dc=1)
    up3, down3 = move(up2, dz=1), move(down2, dz=-1)
    far_up, far_down = cut(up3, down3)
    far_up, far_down = move(far_up, dz=1), move(far_down, dz=-1)
    payloads = (pay, up1, down1, up2, down2, up3, down3)
    requests = [p[HALF : HALF + REQUEST, :HD] for p in payloads]
    tables = len(payloads)
    near = make_lists(
        position,
        jnp.concatenate(requests, axis=0),
        0,
        tables,
        tuple((table, 0, BLOCKS) for table in range(tables)),
    )
    far_k, far_v, *near = barrier((far_k, far_v, *near))
    far_k_twin, far_v_twin = move(far_k, dc=1), move(far_v, dc=1)
    key_refs = (own, own_twin, right, right_twin, far_k, far_k_twin, left, left_twin)
    value_refs = (own, own_twin, right, right_twin, far_v, far_v_twin, left, left_twin)
    plane = (*gather_means(key_refs), key_refs, value_refs)
    far_up, far_down = barrier((far_up, far_down))
    both, mid = (0, HALF + REQUEST), BLOCKS // 2
    far = make_lists(position, far_up, HALF, 1, ((0, 0, mid), (0, mid, BLOCKS)))

    up_a, down_b = part(
        plane, *far, (far_up, far_down), (((0,), 0, mid, 0, 0), ((REQUEST,), mid, mid, 1, 0))
    )
    up_a, down_b = move(up_a, dz=-1), move(down_b, dz=1)
    up_b = down_a = None
    for hop, up, down in ((3, up3, down3), (2, up2, down2), (1, up1, down1)):
        first = 2 * hop - 1
        groups = tuple((both, 0, BLOCKS, first + i, first + i) for i in range(2))
        own_up_a, own_up_b, own_down_a, own_down_b = part(plane, *near, (up, down), groups)
        if up_b is None:
            up_b, down_a = own_up_b, own_down_a
        else:
            up_b, down_a = merge((own_up_b, own_down_a), (up_b, down_a))
        up_b, down_a = move(up_b, dz=-1), move(down_a, dz=1)
        up_a, down_b = merge((own_up_a, own_down_b), (up_a, down_b))
        up_a, down_b = move(up_a, dz=-1), move(down_b, dz=1)
    own_a, own_b = part(plane, *near, (pay,), ((both, 0, BLOCKS, 0, 0),))
    return last((own_a, own_b, up_a, up_b, down_a, down_b))


def solution(mesh):
    placed = (P("ctx", "head"), P("ctx", "head"), P("ctx", "head"), P("ctx", None), P("ctx"))
    return jax.shard_map(
        body, mesh=mesh, in_specs=placed, out_specs=P("ctx", "head"), check_vma=False
    )
```
